512 devices in a mesh: grp: 16 (over z, y_hi), head: 32 (over y_lo, x, core).
Axes of the slice: x: 4, y: 8 (y_hi: 2, y_lo: 4; y = y_hi * 4 + y_lo), z: 8, core: 2. Of those that a mesh axis runs over, the one named last changes fastest.
Arguments:
- cache: bfloat16 [512, 2, 8, 128, 128], P(('grp', 'head')), parts along dimension 0, may hold values from -6 to 6
- fresh: bfloat16 [512, 3, 2, 8, 128], P(('grp', 'head')), parts along dimension 0, may hold values from -6 to 6
- slot_map: int32 [1024], P('grp'), parts along dimension 0, may hold values from 0 to 7, as said below
- lengths: int32 [64], P('grp'), parts along dimension 0, may hold values from 1 to 128, 256 in all
- out_weight: bfloat16 [8192, 6144], P('head'), may hold values from -1.5 to 1.5
- residual: bfloat16 [64, 2, 6144], P('grp', None, 'head'), parts along dimension 0, may hold values from -6 to 6
- norm_gain: float32 [6144], replicated, may hold values from 0.25 to 1.75
- norm_bias: float32 [6144], replicated, may hold values from -3 to 3
Outputs:
- cache_new: bfloat16 [512, 4, 2, 2, 128, 128], P(('grp', 'head')), parts along dimension 0
- hidden: bfloat16 [64, 2, 6144], P('grp', None, 'head'), parts along dimension 0
- normed: bfloat16 [64, 2, 6144], P('grp'), parts along dimension 0
The draws below stay inside these ranges and needn't reach their ends.
There are 16 independent parts, one for each index of `grp`. The reference program is written for one: setup_inputs(seed, part) draws one part's arguments, and reference() takes and returns one part's arrays. A program takes and returns all parts, laid end to end along the dimension named above; an argument that names none is the same for every part. Nothing has to cross between parts.
Inputs may be any that keep to these rules, and one draw needn't show every extreme that they name: `slot_map`: for each old member m, the entries of the new members r * 8 + m (r below 4) together take each of its 8 slots once.
All inputs are finite; a program needn't handle non-finite values.
Results may differ from the reference program's by a relative error of at most 0.0061.
Values may be sent and summed in bfloat16 or wider, within the bound.
No kernel may reach another device: no remote copies, remote signals or barrier semaphores. Data moves between devices by JAX's collectives and lax.ppermute only.
A program may use at most 64 MiB of HBM per device.

```python
import math
import jax
import jax.numpy as jnp
import numpy as np
from jax import lax

ROWS = 4
HEAD_DEV = 2
HEAD_DIM = 128
LEN = 128
OUT = 6144
LANES = 32
SLOTS = 8
FEATURES = 8192
N_HEAD = 32


def draw_cache(key, part):
    key = jax.random.fold_in(key, 1)
    shape = (LANES, 2, SLOTS, LEN, HEAD_DIM)
    base = jnp.clip(jax.random.normal(key, shape), -6.0, 6.0)
    return base.astype(jnp.bfloat16)


def draw_fresh(key, part):
    key = jax.random.fold_in(key, 2)
    shape = (LANES, 3, 2, SLOTS, HEAD_DIM)
    base = jnp.clip(jax.random.normal(key, shape), -6.0, 6.0)
    return base.astype(jnp.bfloat16)


def draw_slot_map(key, part):
    key = jax.random.fold_in(key, 3)
    keys = jax.random.split(key, LANES // ROWS)
    perms = jax.vmap(lambda single: jax.random.permutation(single, SLOTS))(keys)
    perms = perms.reshape(LANES // ROWS, ROWS, HEAD_DEV)
    return jnp.transpose(perms, (1, 0, 2)).reshape(-1).astype(jnp.int32)


def raised(values, rng, source, target, parts, factor):
    def block_of(axis_at):
        return (jnp.arange(values.shape[axis_at]) // (values.shape[axis_at] // parts)).reshape((-1,) + (1,) * (values.ndim - 1 - axis_at))

    first = jax.random.permutation(rng, parts)[block_of(target)]
    far = (block_of(target) + parts // 2) % parts
    return jnp.where((block_of(source) == first) | (block_of(source) == far), factor * values, values)


def steps_of(rng, extent, cuts, smallest, top_value):
    level, own = 1.0, jax.random.fold_in(rng, 6)
    for position, blocks in cuts:
        steps = jnp.exp(jax.random.uniform(jax.random.fold_in(own, position), (blocks,), jnp.float32, smallest / len(cuts), top_value / len(cuts)))
        level = level * jnp.repeat(steps, extent[position] // blocks).reshape([-1 if axis == position else 1 for axis in range(len(extent))])
    return level


def profile(count, total, reach, slope):
    loads = [(1 << 20) // math.isqrt(standing ** slope) + 1 for standing in range(2, count + 1)]
    rest, given = total - reach - (count - 1), [1] * (count - 1)
    while rest > 0:
        movable = [i for i in range(count - 1) if given[i] < reach]
        pool, remaining = sum([loads[i] for i in movable]), rest
        for i in movable:
            extra = min(reach - given[i], max(1, remaining * loads[i] // pool), rest)
            given[i] = given[i] + extra
            rest = rest - extra
    return np.array([reach] + given)


def uneven(stream_key, amount, total, most, lean):
    if amount == 2:
        one = jax.random.randint(stream_key, (), max(1, total - most), min(most, total - 1) + 1)
        return jnp.stack([one, total - one])
    tallies = jnp.asarray(profile(amount, total, most, lean), jnp.int32)
    pairs = (amount - 1) // 2
    donor, taker = tallies[1:1 + 2 * pairs:2], tallies[2:2 + 2 * pairs:2]
    slack = jnp.minimum(donor - 1, most - taker)
    moved = jax.random.randint(jax.random.fold_in(stream_key, 1), (pairs,), 0, 1 << 20) % (slack + 1)
    tallies = tallies.at[1:1 + 2 * pairs:2].set(donor - moved).at[2:2 + 2 * pairs:2].set(taker + moved)
    return tallies[jax.random.permutation(jax.random.fold_in(stream_key, 2), amount)]


def scatter_about(stream_key, shape, deviation, most, cuts=(), kind=jnp.bfloat16):
    loudness = steps_of(stream_key, shape, cuts, -0.22, 0.18) if cuts else 1.0
    entries = jax.random.normal(stream_key, shape, jnp.float32) * deviation * loudness
    return jnp.minimum(jnp.maximum(entries, -most), most).astype(kind)


def noise_with(key, dims, width, most, pieces, heavy, held_as=jnp.bfloat16):
    values = width * jax.random.normal(key, dims, jnp.float32)
    if pieces:
        values = values * steps_of(key, dims, pieces, -0.22, 0.18)
    return jnp.clip(raised(values, jax.random.fold_in(key, 3), *heavy), -most, most).astype(held_as)


def setup_inputs(seed: int = 0, part: int = 0) -> dict:
    key_of = jax.random.split(jax.random.key(seed), 9)
    part_keys = jax.random.split(jax.random.fold_in(key_of[8], part), 9)
    cache = draw_cache(jax.random.fold_in(jax.random.fold_in(key_of[8], part), 71), part)
    fresh = draw_fresh(jax.random.fold_in(jax.random.fold_in(key_of[8], part), 71), part)
    slot_map = draw_slot_map(jax.random.fold_in(jax.random.fold_in(key_of[8], part), 71), part)
    lengths = uneven(part_keys[3], ROWS, 2 * LEN, LEN, 1).astype(jnp.int32)
    out_weight = noise_with(key_of[4], (FEATURES, OUT), (HEAD_DIM // 2) ** -0.5, 1.5, ((0, 32),), (0, 1, 32, 2.75))
    residual = scatter_about(part_keys[5], (ROWS, 2, OUT), 1.0, 6.0, ((2, 32),))
    norm_gain = jnp.clip(1.0 + 0.15 * jax.random.normal(key_of[6], (OUT,), jnp.float32), 0.25, 1.75)
    norm_bias = scatter_about(key_of[7], (OUT,), 0.5, 3.0, (), jnp.float32)
    return dict(cache=cache, fresh=fresh, slot_map=slot_map, lengths=lengths, out_weight=out_weight, residual=residual, norm_gain=norm_gain, norm_bias=norm_bias)


def attend(kv_block, fresh_block, lens):
    keys = kv_block[:, 0].astype(jnp.float32)
    vals = kv_block[:, 1].astype(jnp.float32)
    query = fresh_block[:, 0].astype(jnp.float32)
    new_keys = fresh_block[:, 1].astype(jnp.float32)
    new_vals = fresh_block[:, 2].astype(jnp.float32)
    scale = 1.0 / math.sqrt(keys.shape[-1])
    positions = jnp.arange(keys.shape[2], dtype=jnp.int32)
    visible = positions[None, None, :] < lens[:, None, None]
    results = []
    for step in range(2):
        single = query[:, step]
        old_scores = jnp.einsum('bhd,bhpd->bhp', single, keys) * scale
        old_scores = jnp.where(visible, old_scores, -1e+30)
        new_scores = jnp.einsum('bhd,buhd->bhu', single, new_keys) * scale
        new_scores = jnp.where(jnp.arange(2)[None, None, :] <= step, new_scores, -1e+30)
        top = jnp.maximum(old_scores.max(-1), new_scores.max(-1))[..., None]
        old_exp = jnp.where(visible, jnp.exp(old_scores - top), 0.0)
        new_exp = jnp.where(jnp.arange(2)[None, None, :] <= step, jnp.exp(new_scores - top), 0.0)
        total = old_exp.sum(-1, keepdims=True) + new_exp.sum(-1, keepdims=True)
        old_w = (old_exp / total).astype(jnp.bfloat16).astype(jnp.float32)
        new_w = (new_exp / total).astype(jnp.bfloat16).astype(jnp.float32)
        result = jnp.einsum('bhp,bhpd->bhd', old_w, vals) + jnp.einsum('bhu,buhd->bhd', new_w, new_vals)
        results.append(result)
    return jnp.stack(results, axis=1)

def reference(cache, fresh, slot_map, lengths, out_weight, residual, norm_gain, norm_bias):
    old_count = N_HEAD // ROWS
    lane_rows = jnp.arange(N_HEAD, dtype=jnp.int32) // old_count
    attended = attend(cache, fresh, lengths[lane_rows]).astype(jnp.bfloat16)
    members = jnp.arange(N_HEAD, dtype=jnp.int32)
    lane_index = jnp.arange(ROWS, dtype=jnp.int32)[:, None] * old_count + members[None, :] % old_count
    slots = slot_map.reshape(N_HEAD, HEAD_DEV)
    moved = jnp.take_along_axis(cache[lane_index], slots[None, :, None, :, None, None], axis=3)
    cache_new = jnp.transpose(moved, (1, 0, 2, 3, 4, 5))
    picked = attended[lane_index]
    chosen = jnp.take_along_axis(picked, slots[None, :, None, :, None], axis=3)
    features = jnp.transpose(chosen, (0, 2, 1, 3, 4)).reshape(ROWS * 2, N_HEAD * HEAD_DEV * HEAD_DIM)
    projected = jnp.dot(features, out_weight, preferred_element_type=jnp.float32)
    hidden = (residual.reshape(ROWS * 2, OUT).astype(jnp.float32) + projected).astype(jnp.bfloat16)
    values = hidden.astype(jnp.float32)
    mean = lax.optimization_barrier(jnp.mean(values, axis=-1, keepdims=True))
    var = lax.optimization_barrier(jnp.mean((values - mean) ** 2, axis=-1, keepdims=True))
    normed = ((values - mean) / jnp.sqrt(var + 1e-05) * norm_gain + norm_bias).astype(jnp.bfloat16)
    return (cache_new, hidden.reshape(ROWS, 2, OUT), normed.reshape(ROWS, 2, OUT))
```

```python
import math

import jax
import jax.numpy as jnp
from jax import lax
from jax.experimental import pallas as pl
from jax.experimental.pallas import tpu as pltpu
from jax.sharding import PartitionSpec as P

ROWS = 4
HEAD_DEV = 2
HEAD_DIM = 128
SLOTS = 8
LEN = 128
OUT = 6144
MEMBERS = 32
OLD = MEMBERS // ROWS
SHARE = OUT // MEMBERS
F32 = jnp.float32
BF16 = jnp.bfloat16


def attend_kernel(slot_ref, len_ref, cache_ref, fresh_ref, att_ref, kv_ref, att_scr, sems):
    me = lax.axis_index("head")
    row = me // OLD
    lane = me % OLD
    copies = []
    for target in range(ROWS):
        for i in range(HEAD_DEV):
            slot = slot_ref[(target * OLD + lane) * HEAD_DEV + i]
            for kind in range(2):
                copy = pltpu.make_async_copy(
                    cache_ref.at[0, kind, slot], kv_ref.at[target, kind, i], sems.at[len(copies)]
                )
                copy.start()
                copies.append(copy)
    length = len_ref[row]
    scale = 1.0 / math.sqrt(HEAD_DIM)
    query_rows, old_scores, new_first, new_second = [], [], [], []
    odd = lax.broadcasted_iota(jnp.int32, (8, HEAD_DIM), 0) % 2 == 1
    fresh = fresh_ref[0].astype(F32)
    for slot in range(SLOTS):
        query = jnp.where(
            odd,
            jnp.broadcast_to(fresh[0, 1, slot : slot + 1], (8, HEAD_DIM)),
            jnp.broadcast_to(fresh[0, 0, slot : slot + 1], (8, HEAD_DIM)),
        )
        query_rows.append(query)
        old_scores.append(
            lax.dot_general(
                query.astype(BF16),
                cache_ref[0, 0, slot],
                (((1,), (1,)), ((), ())),
                preferred_element_type=F32,
            )
        )
        new_first.append(jnp.sum(query * fresh[1, 0, slot : slot + 1], axis=-1, keepdims=True))
        new_second.append(jnp.sum(query * fresh[1, 1, slot : slot + 1], axis=-1, keepdims=True))
    shape = (SLOTS * 8, LEN)
    scores = jnp.concatenate(old_scores, axis=0) * scale
    first = jnp.concatenate(new_first, axis=0) * scale
    second = jnp.concatenate(new_second, axis=0) * scale
    visible = lax.broadcasted_iota(jnp.int32, shape, 1) < length
    later = lax.broadcasted_iota(jnp.int32, (SLOTS * 8, 1), 0) % 2 == 1
    scores = jnp.where(visible, scores, -1e30)
    second = jnp.where(later, second, -1e30)
    top = jnp.maximum(jnp.max(scores, axis=-1, keepdims=True), jnp.maximum(first, second))
    old_exp = jnp.where(visible, jnp.exp(scores - top), 0.0)
    first_exp = jnp.exp(first - top)
    second_exp = jnp.where(later, jnp.exp(second - top), 0.0)
    total = jnp.sum(old_exp, axis=-1, keepdims=True) + first_exp + second_exp
    old_w = (old_exp / total).astype(BF16)
    first_w = (first_exp / total).astype(BF16).astype(F32)
    second_w = (second_exp / total).astype(BF16).astype(F32)
    mine = lax.broadcasted_iota(jnp.int32, (8, HEAD_DIM), 0) // 2 == row
    for slot in range(SLOTS):
        part = slice(slot * 8, slot * 8 + 8)
        result = jnp.dot(old_w[part], cache_ref[0, 1, slot], preferred_element_type=F32)
        result = result + (
            first_w[part] * fresh[2, 0, slot : slot + 1]
            + second_w[part] * fresh[2, 1, slot : slot + 1]
        )
        att_scr[slot] = jnp.where(mine, result, 0.0)
    for target in range(ROWS):
        pair = [
            att_scr[slot_ref[(target * OLD + lane) * HEAD_DEV + i]] for i in range(HEAD_DEV)
        ]
        att_ref[target] = jnp.concatenate(pair, axis=0).astype(BF16)
    for copy in copies:
        copy.wait()


def attend_and_pick(slot_map, lengths, cache, fresh):
    smem = pl.BlockSpec(memory_space=pltpu.SMEM)
    vmem = pl.BlockSpec(memory_space=pltpu.VMEM)
    return pl.pallas_call(
        attend_kernel,
        out_shape=(
            jax.ShapeDtypeStruct((ROWS, HEAD_DEV * 8, HEAD_DIM), BF16),
            jax.ShapeDtypeStruct((ROWS, 2, HEAD_DEV, LEN, HEAD_DIM), BF16),
        ),
        in_specs=[smem, smem, vmem, vmem],
        out_specs=(vmem, pl.BlockSpec(memory_space=pl.ANY)),
        scratch_shapes=[
            pltpu.VMEM((SLOTS, 8, HEAD_DIM), F32),
            pltpu.SemaphoreType.DMA((ROWS * HEAD_DEV * 2,)),
        ],
        compiler_params=pltpu.CompilerParams(vmem_limit_bytes=16 * 2**20),
        name="attend_and_pick",
    )(slot_map, lengths, cache, fresh)


CHUNK = 2 * SHARE
CHUNKS = OUT // CHUNK


def project_kernel(att_ref, weight_ref, out_ref):
    total = att_ref[0].astype(F32)
    for row in range(1, ROWS):
        total = total + att_ref[row].astype(F32)
    features = jnp.concatenate([total[:8], total[8:]], axis=1).astype(BF16)
    for chunk in range(CHUNKS):
        part = jnp.dot(
            features,
            weight_ref[:, chunk * CHUNK : (chunk + 1) * CHUNK],
            preferred_element_type=F32,
        )
        out_ref[2 * chunk] = part[:, :SHARE].astype(BF16)
        out_ref[2 * chunk + 1] = part[:, SHARE:].astype(BF16)


def project(attended, out_weight):
    vmem = pl.BlockSpec(memory_space=pltpu.VMEM)
    return pl.pallas_call(
        project_kernel,
        out_shape=jax.ShapeDtypeStruct((MEMBERS, 8, SHARE), BF16),
        in_specs=[vmem, vmem],
        out_specs=vmem,
        compiler_params=pltpu.CompilerParams(vmem_limit_bytes=16 * 2**20),
        name="project",
    )(attended, out_weight)


def add_kernel(parts_ref, residual_ref, hidden_ref, spread_ref):
    total = parts_ref[0].astype(F32)
    for member in range(1, MEMBERS):
        total = total + parts_ref[member].astype(F32)
    hidden = (residual_ref[...].astype(F32) + total).astype(BF16)
    hidden_ref[...] = hidden
    for member in range(MEMBERS):
        spread_ref[member] = hidden


def add_residual(parts, residual):
    vmem = pl.BlockSpec(memory_space=pltpu.VMEM)
    return pl.pallas_call(
        add_kernel,
        out_shape=(
            jax.ShapeDtypeStruct((8, SHARE), BF16),
            jax.ShapeDtypeStruct((MEMBERS, 8, SHARE), BF16),
        ),
        in_specs=[vmem, vmem],
        out_specs=(vmem, vmem),
        compiler_params=pltpu.CompilerParams(vmem_limit_bytes=16 * 2**20),
        name="add_residual",
    )(parts, residual)


def norm_kernel(blocks_ref, gain_ref, bias_ref, out_ref):
    total = blocks_ref[0].astype(F32)
    for member in range(1, MEMBERS):
        total = total + blocks_ref[member].astype(F32)
    mean = jnp.sum(total, axis=-1, keepdims=True) / OUT
    spread = jnp.zeros((8, SHARE), F32)
    for member in range(MEMBERS):
        spread = spread + (blocks_ref[member].astype(F32) - mean) ** 2
    var = jnp.sum(spread, axis=-1, keepdims=True) / OUT
    scale = 1.0 / jnp.sqrt(var + 1e-05)
    for chunk in range(CHUNKS):
        values = jnp.concatenate(
            [blocks_ref[2 * chunk].astype(F32), blocks_ref[2 * chunk + 1].astype(F32)], axis=1
        )
        values = (values - mean) * scale
        for tile in range(CHUNK // 128):
            at = chunk * (CHUNK // 128) + tile
            part = values[:, tile * 128 : (tile + 1) * 128]
            part = part * gain_ref[at : at + 1] + bias_ref[at : at + 1]
            out_ref[:, at * 128 : (at + 1) * 128] = part.astype(BF16)


def normalize(blocks, gain, bias):
    vmem = pl.BlockSpec(memory_space=pltpu.VMEM)
    return pl.pallas_call(
        norm_kernel,
        out_shape=jax.ShapeDtypeStruct((8, OUT), BF16),
        in_specs=[vmem, vmem, vmem],
        out_specs=vmem,
        compiler_params=pltpu.CompilerParams(vmem_limit_bytes=16 * 2**20),
        name="normalize",
    )(blocks, gain.reshape(OUT // 128, 128), bias.reshape(OUT // 128, 128))


def exchange(blocks, groups=None):
    return lax.all_to_all(blocks, "head", 0, 0, axis_index_groups=groups, tiled=True)


def body(cache, fresh, slot_map, lengths, out_weight, residual, norm_gain, norm_bias):
    columns = [[row * OLD + lane for row in range(ROWS)] for lane in range(OLD)]
    picked, kv_blocks = attend_and_pick(slot_map, lengths, cache, fresh)
    attended = exchange(picked, columns)
    cache_new = exchange(kv_blocks, columns)[None]
    parts = exchange(project(attended, out_weight))
    hidden, copies = add_residual(parts, residual.reshape(ROWS * 2, SHARE))
    normed = normalize(exchange(copies), norm_gain, norm_bias)
    return (cache_new, hidden.reshape(ROWS, 2, SHARE), normed.reshape(ROWS, 2, OUT))


def solution(mesh):
    in_specs = (
        P(("grp", "head"), None, None, None, None),
        P(("grp", "head"), None, None, None, None),
        P("grp"),
        P("grp"),
        P("head", None),
        P("grp", None, "head"),
        P(),
        P(),
    )
    out_specs = (
        P(("grp", "head"), None, None, None, None, None),
        P("grp", None, "head"),
        P("grp", None, None),
    )
    return jax.shard_map(body, mesh=mesh, in_specs=in_specs, out_specs=out_specs, check_vma=False)
```

```python
import math

import jax
import jax.numpy as jnp
from jax import lax
from jax.experimental import pallas as pl
from jax.experimental.pallas import tpu as pltpu
from jax.sharding import PartitionSpec as P

ROWS = 4
HEAD_DEV = 2
HEAD_DIM = 128
SLOTS = 8
LEN = 128
OUT = 6144
MEMBERS = 32
CORES = 2
CHIPS = MEMBERS // CORES
OLD = MEMBERS // ROWS
SHARE = OUT // MEMBERS
CHUNK = OUT // CHIPS
F32 = jnp.float32
BF16 = jnp.bfloat16
FIRST_LIMIT = 56 * 2**20
VMEM_LIMIT = 8 * 2**20
SMEM = pl.BlockSpec(memory_space=pltpu.SMEM)
VMEM = pl.BlockSpec(memory_space=pltpu.VMEM)
ANY = pl.BlockSpec(memory_space=pl.ANY)


def attend_kernel(
    slot_ref, len_ref, cache_ref, fresh_ref, att_ref, new_ref, kv1, kv2, kv3, held, att_scr, in_sems, sems
):
    me = lax.axis_index("head")
    row = me // OLD
    lane = me % OLD
    loads = []
    for kind in range(2):
        load = pltpu.make_async_copy(cache_ref.at[0, kind], held.at[kind], in_sems.at[kind])
        load.start()
        loads.append(load)
    copies = []

    def pick(kind):
        for offset, kv_ref in ((1, kv1), (2, kv2), (3, kv3), (0, new_ref.at[0, row])):
            target = (row + offset) % ROWS
            for i in range(HEAD_DEV):
                slot = slot_ref[(target * OLD + lane) * HEAD_DEV + i]
                copy = pltpu.make_async_copy(
                    held.at[kind, slot], kv_ref.at[kind, i], sems.at[len(copies)]
                )
                copy.start()
                copies.append(copy)

    length = len_ref[row]
    scale = 1.0 / math.sqrt(HEAD_DIM)
    query_rows, old_scores, new_first, new_second = [], [], [], []
    odd = lax.broadcasted_iota(jnp.int32, (8, HEAD_DIM), 0) % 2 == 1
    fresh = fresh_ref[0].astype(F32)
    for slot in range(SLOTS):
        query = jnp.where(
            odd,
            jnp.broadcast_to(fresh[0, 1, slot : slot + 1], (8, HEAD_DIM)),
            jnp.broadcast_to(fresh[0, 0, slot : slot + 1], (8, HEAD_DIM)),
        )
        query_rows.append(query.astype(BF16))
        new_first.append(jnp.sum(query * fresh[1, 0, slot : slot + 1], axis=-1, keepdims=True))
        new_second.append(jnp.sum(query * fresh[1, 1, slot : slot + 1], axis=-1, keepdims=True))
    loads[0].wait()
    pick(0)
    for slot in range(SLOTS):
        old_scores.append(
            lax.dot_general(
                query_rows[slot],
                held[0, slot],
                (((1,), (1,)), ((), ())),
                preferred_element_type=F32,
            )
        )
    shape = (SLOTS * 8, LEN)
    scores = jnp.concatenate(old_scores, axis=0) * scale
    first = jnp.concatenate(new_first, axis=0) * scale
    second = jnp.concatenate(new_second, axis=0) * scale
    visible = lax.broadcasted_iota(jnp.int32, shape, 1) < length
    later = lax.broadcasted_iota(jnp.int32, (SLOTS * 8, 1), 0) % 2 == 1
    scores = jnp.where(visible, scores, -1e30)
    second = jnp.where(later, second, -1e30)
    top = jnp.maximum(jnp.max(scores, axis=-1, keepdims=True), jnp.maximum(first, second))
    old_exp = jnp.where(visible, jnp.exp(scores - top), 0.0)
    first_exp = jnp.exp(first - top)
    second_exp = jnp.where(later, jnp.exp(second - top), 0.0)
    total = jnp.sum(old_exp, axis=-1, keepdims=True) + first_exp + second_exp
    old_w = (old_exp / total).astype(BF16)
    first_w = (first_exp / total).astype(BF16).astype(F32)
    second_w = (second_exp / total).astype(BF16).astype(F32)
    mine = lax.broadcasted_iota(jnp.int32, (8, HEAD_DIM), 0) // 2 == row
    loads[1].wait()
    pick(1)
    for slot in range(SLOTS):
        part = slice(slot * 8, slot * 8 + 8)
        result = jnp.dot(old_w[part], held[1, slot], preferred_element_type=F32)
        result = result + (
            first_w[part] * fresh[2, 0, slot : slot + 1]
            + second_w[part] * fresh[2, 1, slot : slot + 1]
        )
        att_scr[slot] = jnp.where(mine, result, 0.0)
    for target in range(ROWS):
        pair = [
            att_scr[slot_ref[(target * OLD + lane) * HEAD_DEV + i]] for i in range(HEAD_DEV)
        ]
        att_ref[target] = jnp.concatenate(pair, axis=0).astype(BF16)
    for copy in copies:
        copy.wait()


def attend_and_pick(slot_map, lengths, cache, fresh):
    block = (2, HEAD_DEV, LEN, HEAD_DIM)
    return pl.pallas_call(
        attend_kernel,
        out_shape=(
            jax.ShapeDtypeStruct((ROWS, HEAD_DEV * 8, HEAD_DIM), BF16),
            jax.ShapeDtypeStruct((1, ROWS) + block, BF16),
            *[jax.ShapeDtypeStruct(block, BF16)] * (ROWS - 1),
        ),
        in_specs=[SMEM, SMEM, ANY, VMEM],
        out_specs=(VMEM, *[ANY] * ROWS),
        scratch_shapes=[
            pltpu.VMEM((2, SLOTS, LEN, HEAD_DIM), BF16),
            pltpu.VMEM((SLOTS, 8, HEAD_DIM), F32),
            pltpu.SemaphoreType.DMA((2,)),
            pltpu.SemaphoreType.DMA((ROWS * HEAD_DEV * 2,)),
        ],
        compiler_params=pltpu.CompilerParams(vmem_limit_bytes=FIRST_LIMIT),
        name="attend_and_pick",
    )(slot_map, lengths, cache, fresh)


def project_kernel(att_ref, weight_ref, out_ref):
    total = att_ref[0].astype(F32)
    for row in range(1, ROWS):
        total = total + att_ref[row].astype(F32)
    features = jnp.concatenate([total[:8], total[8:]], axis=1).astype(BF16)
    for chip in range(CHIPS):
        part = jnp.dot(
            features,
            weight_ref[:, chip * CHUNK : (chip + 1) * CHUNK],
            preferred_element_type=F32,
        )
        out_ref[chip] = part.astype(BF16)


def project(attended, out_weight):
    return pl.pallas_call(
        project_kernel,
        out_shape=jax.ShapeDtypeStruct((CHIPS, 8, CHUNK), BF16),
        in_specs=[VMEM, VMEM],
        out_specs=VMEM,
        compiler_params=pltpu.CompilerParams(vmem_limit_bytes=VMEM_LIMIT),
        name="project",
    )(attended, out_weight)


def add_kernel(parts_ref, residual_ref, out_ref):
    core = lax.axis_index("head") % CORES
    total = parts_ref[0].astype(F32)
    for chip in range(1, CHIPS):
        total = total + parts_ref[chip].astype(F32)
    own = jnp.concatenate([residual_ref[row].astype(F32) for row in range(ROWS)], axis=0)
    none = jnp.zeros_like(own)
    own = jnp.concatenate(
        [jnp.where(core == 0, own, none), jnp.where(core == 1, own, none)], axis=1
    )
    out_ref[...] = total + own


def add_residual(parts, residual):
    return pl.pallas_call(
        add_kernel,
        out_shape=jax.ShapeDtypeStruct((8, CHUNK), F32),
        in_specs=[VMEM, VMEM],
        out_specs=VMEM,
        compiler_params=pltpu.CompilerParams(vmem_limit_bytes=VMEM_LIMIT),
        name="add_residual",
    )(parts, residual)


def hidden_kernel(sums_ref, hidden_ref, spread_ref):
    core = lax.axis_index("head") % CORES
    total = sums_ref[0] + sums_ref[1]
    hidden = total.astype(BF16)
    own = jnp.where(core == 0, total[:, :SHARE], total[:, SHARE:]).astype(BF16)
    for row in range(ROWS):
        hidden_ref[row] = own[2 * row : 2 * row + 2]
    for chip in range(CHIPS):
        spread_ref[chip] = hidden


def round_hidden(sums):
    return pl.pallas_call(
        hidden_kernel,
        out_shape=(
            jax.ShapeDtypeStruct((ROWS, 2, SHARE), BF16),
            jax.ShapeDtypeStruct((CHIPS, 8, CHUNK), BF16),
        ),
        in_specs=[VMEM],
        out_specs=(VMEM, VMEM),
        compiler_params=pltpu.CompilerParams(vmem_limit_bytes=VMEM_LIMIT),
        name="round_hidden",
    )(sums)


def norm_kernel(blocks_ref, gain_ref, bias_ref, kv1, kv2, kv3, _, out_ref, cache_ref, sems):
    row = lax.axis_index("head") // OLD
    copies = []
    for offset, kv_ref in enumerate((kv1, kv2, kv3), 1):
        source = (row + ROWS - offset) % ROWS
        copy = pltpu.make_async_copy(kv_ref, cache_ref.at[0, source], sems.at[offset - 1])
        copy.start()
        copies.append(copy)
    total = blocks_ref[0].astype(F32)
    for chip in range(1, CHIPS):
        total = total + blocks_ref[chip].astype(F32)
    mean = jnp.sum(total, axis=-1, keepdims=True) / OUT
    spread = jnp.zeros((8, CHUNK), F32)
    for chip in range(CHIPS):
        spread = spread + (blocks_ref[chip].astype(F32) - mean) ** 2
    var = jnp.sum(spread, axis=-1, keepdims=True) / OUT
    scale = 1.0 / jnp.sqrt(var + 1e-05)
    tiles = CHUNK // 128
    for chip in range(CHIPS):
        values = (blocks_ref[chip].astype(F32) - mean) * scale
        for tile in range(tiles):
            at = chip * tiles + tile
            part = values[:, tile * 128 : (tile + 1) * 128]
            part = (part * gain_ref[at : at + 1] + bias_ref[at : at + 1]).astype(BF16)
            for step in range(ROWS):
                out_ref[step, :, at * 128 : (at + 1) * 128] = part[2 * step : 2 * step + 2]
    for copy in copies:
        copy.wait()


def normalize(blocks, gain, bias, kv, cache_new):
    return pl.pallas_call(
        norm_kernel,
        out_shape=(
            jax.ShapeDtypeStruct((ROWS, 2, OUT), BF16),
            jax.ShapeDtypeStruct(cache_new.shape, BF16),
        ),
        in_specs=[VMEM] * 6 + [ANY],
        out_specs=(VMEM, ANY),
        scratch_shapes=[pltpu.SemaphoreType.DMA((ROWS - 1,))],
        input_output_aliases={6: 1},
        compiler_params=pltpu.CompilerParams(vmem_limit_bytes=VMEM_LIMIT),
        name="normalize",
    )(blocks, gain.reshape(OUT // 128, 128), bias.reshape(OUT // 128, 128), *kv, cache_new)


def exchange(blocks, groups):
    return lax.all_to_all(blocks, "head", 0, 0, axis_index_groups=groups, tiled=True)


def body(cache, fresh, slot_map, lengths, out_weight, residual, norm_gain, norm_bias):
    columns = [[row * OLD + lane for row in range(ROWS)] for lane in range(OLD)]
    sides = [[chip * CORES + core for chip in range(CHIPS)] for core in range(CORES)]
    pairs = [[chip * CORES + core for core in range(CORES)] for chip in range(CHIPS)]
    picked, cache_new, *kv = attend_and_pick(slot_map, lengths, cache, fresh)
    for offset in range(1, ROWS):
        to = [(i, (i + offset * OLD) % MEMBERS) for i in range(MEMBERS)]
        kv[offset - 1] = lax.ppermute(kv[offset - 1], "head", to)
    parts = exchange(project(exchange(picked, columns), out_weight), sides)
    sums = lax.all_gather(add_residual(parts, residual), "head", axis_index_groups=pairs)
    hidden, copies = round_hidden(sums)
    normed, cache_new = normalize(exchange(copies, sides), norm_gain, norm_bias, kv, cache_new)
    return (cache_new, hidden, normed)


def solution(mesh):
    in_specs = (
        P(("grp", "head"), None, None, None, None),
        P(("grp", "head"), None, None, None, None),
        P("grp"),
        P("grp"),
        P("head", None),
        P("grp", None, "head"),
        P(),
        P(),
    )
    out_specs = (
        P(("grp", "head"), None, None, None, None, None),
        P("grp", None, "head"),
        P("grp", None, None),
    )
    return jax.shard_map(body, mesh=mesh, in_specs=in_specs, out_specs=out_specs, check_vma=False)
```

```python
import math

import jax
import jax.numpy as jnp
from jax import lax
from jax.experimental import pallas as pl
from jax.experimental.pallas import tpu as pltpu
from jax.sharding import PartitionSpec as P

ROWS = 4
HEAD_DEV = 2
HEAD_DIM = 128
SLOTS = 8
LEN = 128
OUT = 6144
MEMBERS = 32
CORES = 2
CHIPS = MEMBERS // CORES
OLD = MEMBERS // ROWS
SHARE = OUT // MEMBERS
CHUNK = OUT // CHIPS
F32 = jnp.float32
BF16 = jnp.bfloat16
FIRST_LIMIT = 56 * 2**20
VMEM_LIMIT = 8 * 2**20
SMEM = pl.BlockSpec(memory_space=pltpu.SMEM)
VMEM = pl.BlockSpec(memory_space=pltpu.VMEM)
ANY = pl.BlockSpec(memory_space=pl.ANY)


def estimate(microseconds):
    return pl.CostEstimate(
        flops=0, transcendentals=0, bytes_accessed=int(microseconds * 3.69e6)
    )


def attend_kernel(
    slot_hbm, len_hbm, cache_ref, fresh_hbm, att_ref, new_ref, kv1, kv2, kv3,
    slot_scr, len_scr, fresh_scr, held, att_scr, in_sems, sems,
):
    me = lax.axis_index("head")
    row = me // OLD
    lane = me % OLD
    loads = []
    for source, target in (
        (cache_ref.at[0, 0], held.at[0]),
        (fresh_hbm, fresh_scr),
        (slot_hbm, slot_scr),
        (len_hbm, len_scr),
        (cache_ref.at[0, 1], held.at[1]),
    ):
        load = pltpu.make_async_copy(source, target, in_sems.at[len(loads)])
        load.start()
        loads.append(load)
    copies = []

    def pick(kind):
        for offset, kv_ref in ((1, kv1), (2, kv2), (3, kv3), (0, new_ref.at[0, row])):
            target = (row + offset) % ROWS
            for i in range(HEAD_DEV):
                slot = slot_scr[(target * OLD + lane) * HEAD_DEV + i]
                copy = pltpu.make_async_copy(
                    held.at[kind, slot], kv_ref.at[kind, i], sems.at[len(copies)]
                )
                copy.start()
                copies.append(copy)

    scale = 1.0 / math.sqrt(HEAD_DIM)
    query_rows, old_scores, new_first, new_second = [], [], [], []
    odd = lax.broadcasted_iota(jnp.int32, (8, HEAD_DIM), 0) % 2 == 1
    loads[1].wait()
    fresh = fresh_scr[0].astype(F32)
    for slot in range(SLOTS):
        query = jnp.where(
            odd,
            jnp.broadcast_to(fresh[0, 1, slot : slot + 1], (8, HEAD_DIM)),
            jnp.broadcast_to(fresh[0, 0, slot : slot + 1], (8, HEAD_DIM)),
        )
        query_rows.append(query.astype(BF16))
        new_first.append(jnp.sum(query * fresh[1, 0, slot : slot + 1], axis=-1, keepdims=True))
        new_second.append(jnp.sum(query * fresh[1, 1, slot : slot + 1], axis=-1, keepdims=True))
    loads[0].wait()
    loads[2].wait()
    pick(0)
    for slot in range(SLOTS):
        old_scores.append(
            lax.dot_general(
                query_rows[slot],
                held[0, slot],
                (((1,), (1,)), ((), ())),
                preferred_element_type=F32,
            )
        )
    shape = (SLOTS * 8, LEN)
    scores = jnp.concatenate(old_scores, axis=0) * scale
    first = jnp.concatenate(new_first, axis=0) * scale
    second = jnp.concatenate(new_second, axis=0) * scale
    loads[3].wait()
    visible = lax.broadcasted_iota(jnp.int32, shape, 1) < len_scr[row]
    later = lax.broadcasted_iota(jnp.int32, (SLOTS * 8, 1), 0) % 2 == 1
    scores = jnp.where(visible, scores, -1e30)
    second = jnp.where(later, second, -1e30)
    top = jnp.maximum(jnp.max(scores, axis=-1, keepdims=True), jnp.maximum(first, second))
    old_exp = jnp.where(visible, jnp.exp(scores - top), 0.0)
    first_exp = jnp.exp(first - top)
    second_exp = jnp.where(later, jnp.exp(second - top), 0.0)
    total = jnp.sum(old_exp, axis=-1, keepdims=True) + first_exp + second_exp
    old_w = (old_exp / total).astype(BF16)
    first_w = (first_exp / total).astype(BF16).astype(F32)
    second_w = (second_exp / total).astype(BF16).astype(F32)
    mine = lax.broadcasted_iota(jnp.int32, (8, HEAD_DIM), 0) // 2 == row
    loads[4].wait()
    pick(1)
    for slot in range(SLOTS):
        part = slice(slot * 8, slot * 8 + 8)
        result = jnp.dot(old_w[part], held[1, slot], preferred_element_type=F32)
        result = result + (
            first_w[part] * fresh[2, 0, slot : slot + 1]
            + second_w[part] * fresh[2, 1, slot : slot + 1]
        )
        att_scr[slot] = jnp.where(mine, result, 0.0)
    for target in range(ROWS):
        pair = [
            att_scr[slot_scr[(target * OLD + lane) * HEAD_DEV + i]] for i in range(HEAD_DEV)
        ]
        att_ref[target] = jnp.concatenate(pair, axis=0).astype(BF16)
    for copy in copies:
        copy.wait()


def attend_and_pick(slot_map, lengths, cache, fresh):
    block = (2, HEAD_DEV, LEN, HEAD_DIM)
    return pl.pallas_call(
        attend_kernel,
        out_shape=(
            jax.ShapeDtypeStruct((ROWS, HEAD_DEV * 8, HEAD_DIM), BF16),
            jax.ShapeDtypeStruct((1, ROWS) + block, BF16),
            *[jax.ShapeDtypeStruct(block, BF16)] * (ROWS - 1),
        ),
        in_specs=[ANY] * 4,
        out_specs=(VMEM, *[ANY] * ROWS),
        scratch_shapes=[
            pltpu.SMEM(slot_map.shape, jnp.int32),
            pltpu.SMEM(lengths.shape, jnp.int32),
            pltpu.VMEM(fresh.shape, BF16),
            pltpu.VMEM((2, SLOTS, LEN, HEAD_DIM), BF16),
            pltpu.VMEM((SLOTS, 8, HEAD_DIM), F32),
            pltpu.SemaphoreType.DMA((5,)),
            pltpu.SemaphoreType.DMA((ROWS * HEAD_DEV * 2,)),
        ],
        cost_estimate=estimate(3.5),
        compiler_params=pltpu.CompilerParams(vmem_limit_bytes=FIRST_LIMIT),
        name="attend_and_pick",
    )(slot_map, lengths, cache, fresh)


def touch_kernel(weight_ref, out_ref):
    out_ref[...] = weight_ref[:16, :128]


def touch(out_weight):
    return pl.pallas_call(
        touch_kernel,
        out_shape=jax.ShapeDtypeStruct((16, 128), BF16),
        in_specs=[VMEM],
        out_specs=VMEM,
        cost_estimate=estimate(0.2),
        compiler_params=pltpu.CompilerParams(vmem_limit_bytes=VMEM_LIMIT),
        name="touch",
    )(out_weight)


def project_kernel(att_ref, weight_ref, *refs):
    out_ref = refs[-1]
    total = att_ref[0].astype(F32)
    for row in range(1, ROWS):
        total = total + att_ref[row].astype(F32)
    features = jnp.concatenate([total[:8], total[8:]], axis=1).astype(BF16)
    for chip in range(CHIPS):
        part = jnp.dot(
            features,
            weight_ref[:, chip * CHUNK : (chip + 1) * CHUNK],
            preferred_element_type=F32,
        )
        out_ref[chip] = part.astype(BF16)


def project(attended, out_weight, *arrived):
    return pl.pallas_call(
        project_kernel,
        out_shape=jax.ShapeDtypeStruct((CHIPS, 8, CHUNK), BF16),
        in_specs=[VMEM, VMEM] + [ANY] * len(arrived),
        out_specs=VMEM,
        cost_estimate=estimate(0.6),
        compiler_params=pltpu.CompilerParams(vmem_limit_bytes=VMEM_LIMIT),
        name="project",
    )(attended, out_weight, *arrived)


def add_kernel(parts_ref, residual_ref, *refs):
    out_ref = refs[-1]
    core = lax.axis_index("head") % CORES
    total = parts_ref[0].astype(F32)
    for chip in range(1, CHIPS):
        total = total + parts_ref[chip].astype(F32)
    own = jnp.concatenate([residual_ref[row].astype(F32) for row in range(ROWS)], axis=0)
    none = jnp.zeros_like(own)
    own = jnp.concatenate(
        [jnp.where(core == 0, own, none), jnp.where(core == 1, own, none)], axis=1
    )
    out_ref[...] = total + own


def add_residual(parts, residual, *arrived):
    return pl.pallas_call(
        add_kernel,
        out_shape=jax.ShapeDtypeStruct((8, CHUNK), F32),
        in_specs=[VMEM, VMEM] + [ANY] * len(arrived),
        out_specs=VMEM,
        cost_estimate=estimate(0.2),
        compiler_params=pltpu.CompilerParams(vmem_limit_bytes=VMEM_LIMIT),
        name="add_residual",
    )(parts, residual, *arrived)


def hidden_kernel(sums_ref, *refs):
    hidden_ref, spread_ref = refs[-2:]
    core = lax.axis_index("head") % CORES
    total = sums_ref[0] + sums_ref[1]
    hidden = total.astype(BF16)
    own = jnp.where(core == 0, total[:, :SHARE], total[:, SHARE:]).astype(BF16)
    for row in range(ROWS):
        hidden_ref[row] = own[2 * row : 2 * row + 2]
    for chip in range(CHIPS):
        spread_ref[chip] = hidden


def round_hidden(sums, *arrived):
    return pl.pallas_call(
        hidden_kernel,
        out_shape=(
            jax.ShapeDtypeStruct((ROWS, 2, SHARE), BF16),
            jax.ShapeDtypeStruct((CHIPS, 8, CHUNK), BF16),
        ),
        in_specs=[VMEM] + [ANY] * len(arrived),
        out_specs=(VMEM, VMEM),
        cost_estimate=estimate(0.6),
        compiler_params=pltpu.CompilerParams(vmem_limit_bytes=VMEM_LIMIT),
        name="round_hidden",
    )(sums, *arrived)


def norm_kernel(blocks_ref, gain_ref, bias_ref, kv1, kv2, kv3, _, out_ref, cache_ref, sems):
    row = lax.axis_index("head") // OLD
    copies = []
    for offset, kv_ref in enumerate((kv1, kv2, kv3), 1):
        source = (row + ROWS - offset) % ROWS
        copy = pltpu.make_async_copy(kv_ref, cache_ref.at[0, source], sems.at[offset - 1])
        copy.start()
        copies.append(copy)
    total = blocks_ref[0].astype(F32)
    for chip in range(1, CHIPS):
        total = total + blocks_ref[chip].astype(F32)
    mean = jnp.sum(total, axis=-1, keepdims=True) / OUT
    spread = jnp.zeros((8, CHUNK), F32)
    for chip in range(CHIPS):
        spread = spread + (blocks_ref[chip].astype(F32) - mean) ** 2
    var = jnp.sum(spread, axis=-1, keepdims=True) / OUT
    scale = 1.0 / jnp.sqrt(var + 1e-05)
    tiles = CHUNK // 128
    for chip in range(CHIPS):
        values = (blocks_ref[chip].astype(F32) - mean) * scale
        for tile in range(tiles):
            at = chip * tiles + tile
            part = values[:, tile * 128 : (tile + 1) * 128]
            part = (part * gain_ref[at : at + 1] + bias_ref[at : at + 1]).astype(BF16)
            for step in range(ROWS):
                out_ref[step, :, at * 128 : (at + 1) * 128] = part[2 * step : 2 * step + 2]
    for copy in copies:
        copy.wait()


def normalize(blocks, gain, bias, kv, cache_new):
    return pl.pallas_call(
        norm_kernel,
        out_shape=(
            jax.ShapeDtypeStruct((ROWS, 2, OUT), BF16),
            jax.ShapeDtypeStruct(cache_new.shape, BF16),
        ),
        in_specs=[VMEM] * 6 + [ANY],
        out_specs=(VMEM, ANY),
        scratch_shapes=[pltpu.SemaphoreType.DMA((ROWS - 1,))],
        input_output_aliases={6: 1},
        cost_estimate=estimate(1.4),
        compiler_params=pltpu.CompilerParams(vmem_limit_bytes=VMEM_LIMIT),
        name="normalize",
    )(blocks, gain.reshape(OUT // 128, 128), bias.reshape(OUT // 128, 128), *kv, cache_new)


def exchange(blocks, groups):
    return lax.all_to_all(blocks, "head", 0, 0, axis_index_groups=groups, tiled=True)


def body(cache, fresh, slot_map, lengths, out_weight, residual, norm_gain, norm_bias):
    columns = [[row * OLD + lane for row in range(ROWS)] for lane in range(OLD)]
    sides = [[chip * CORES + core for chip in range(CHIPS)] for core in range(CORES)]
    pairs = [[chip * CORES + core for core in range(CORES)] for chip in range(CHIPS)]
    picked, cache_new, *kv = attend_and_pick(slot_map, lengths, cache, fresh)
    for offset in range(1, ROWS):
        to = [(i, (i + offset * OLD) % MEMBERS) for i in range(MEMBERS)]
        kv[offset - 1] = lax.ppermute(kv[offset - 1], "head", to)
    parts = exchange(project(exchange(picked, columns), out_weight, touch(out_weight)), sides)

    def finish(blocks, hidden):
        sums = lax.all_gather(add_residual(blocks, hidden), "head", axis_index_groups=pairs)
        hidden, copies = round_hidden(sums)
        return exchange(copies, sides), hidden

    blocks, hidden = lax.cond(lax.axis_index("head") < MEMBERS, finish, lambda a, b: (a, b), parts, residual)
    normed, cache_new = normalize(blocks, norm_gain, norm_bias, kv, cache_new)
    return (cache_new, hidden, normed)


def solution(mesh):
    in_specs = (
        P(("grp", "head"), None, None, None, None),
        P(("grp", "head"), None, None, None, None),
        P("grp"),
        P("grp"),
        P("head", None),
        P("grp", None, "head"),
        P(),
        P(),
    )
    out_specs = (
        P(("grp", "head"), None, None, None, None, None),
        P("grp", None, "head"),
        P("grp", None, None),
    )
    return jax.shard_map(body, mesh=mesh, in_specs=in_specs, out_specs=out_specs, check_vma=False)
```

```python
import functools
import math

import jax
import jax.numpy as jnp
from jax import lax
from jax.experimental import pallas as pl
from jax.experimental.pallas import tpu as pltpu
from jax.sharding import PartitionSpec as P

ROWS = 4
HEAD_DEV = 2
HEAD_DIM = 128
SLOTS = 8
LEN = 128
OUT = 6144
MEMBERS = 32
CORES = 2
CHIPS = MEMBERS // CORES
OLD = MEMBERS // ROWS
SHARE = OUT // MEMBERS
CHUNK = OUT // CHIPS
F32 = jnp.float32
BF16 = jnp.bfloat16
FIRST_LIMIT = 56 * 2**20
VMEM_LIMIT = 8 * 2**20
SMEM = pl.BlockSpec(memory_space=pltpu.SMEM)
VMEM = pl.BlockSpec(memory_space=pltpu.VMEM)
ANY = pl.BlockSpec(memory_space=pl.ANY)
HBM = pl.BlockSpec(memory_space=pltpu.HBM)


def estimate(microseconds):
    return pl.CostEstimate(
        flops=0, transcendentals=0, bytes_accessed=int(microseconds * 3.69e6)
    )


def attend_kernel(
    slot_hbm, len_hbm, cache_ref, fresh_hbm, att_ref, kv0, kv1, kv2, kv3,
    slot_scr, len_scr, fresh_scr, held, att_scr, in_sems, sems,
):
    me = lax.axis_index("head")
    row = me // OLD
    lane = me % OLD
    loads = []
    for source, target in (
        (cache_ref.at[0, 0], held.at[0]),
        (fresh_hbm, fresh_scr),
        (slot_hbm, slot_scr),
        (len_hbm, len_scr),
        (cache_ref.at[0, 1], held.at[1]),
    ):
        load = pltpu.make_async_copy(source, target, in_sems.at[len(loads)])
        load.start()
        loads.append(load)
    copies = []

    def pick(kind):
        for offset, kv_ref in ((1, kv1), (2, kv2), (3, kv3), (0, kv0)):
            target = (row + offset) % ROWS
            for i in range(HEAD_DEV):
                slot = slot_scr[(target * OLD + lane) * HEAD_DEV + i]
                copy = pltpu.make_async_copy(
                    held.at[kind, slot], kv_ref.at[kind, i], sems.at[len(copies)]
                )
                copy.start()
                copies.append(copy)

    scale = 1.0 / math.sqrt(HEAD_DIM)
    query_rows, old_scores, new_first, new_second = [], [], [], []
    odd = lax.broadcasted_iota(jnp.int32, (8, HEAD_DIM), 0) % 2 == 1
    loads[1].wait()
    fresh = fresh_scr[0].astype(F32)
    for slot in range(SLOTS):
        query = jnp.where(
            odd,
            jnp.broadcast_to(fresh[0, 1, slot : slot + 1], (8, HEAD_DIM)),
            jnp.broadcast_to(fresh[0, 0, slot : slot + 1], (8, HEAD_DIM)),
        )
        query_rows.append(query.astype(BF16))
        new_first.append(jnp.sum(query * fresh[1, 0, slot : slot + 1], axis=-1, keepdims=True))
        new_second.append(jnp.sum(query * fresh[1, 1, slot : slot + 1], axis=-1, keepdims=True))
    loads[0].wait()
    loads[2].wait()
    pick(0)
    for slot in range(SLOTS):
        old_scores.append(
            lax.dot_general(
                query_rows[slot],
                held[0, slot],
                (((1,), (1,)), ((), ())),
                preferred_element_type=F32,
            )
        )
    loads[4].wait()
    pick(1)
    shape = (SLOTS * 8, LEN)
    scores = jnp.concatenate(old_scores, axis=0) * scale
    first = jnp.concatenate(new_first, axis=0) * scale
    second = jnp.concatenate(new_second, axis=0) * scale
    loads[3].wait()
    visible = lax.broadcasted_iota(jnp.int32, shape, 1) < len_scr[row]
    later = lax.broadcasted_iota(jnp.int32, (SLOTS * 8, 1), 0) % 2 == 1
    scores = jnp.where(visible, scores, -1e30)
    second = jnp.where(later, second, -1e30)
    top = jnp.maximum(jnp.max(scores, axis=-1, keepdims=True), jnp.maximum(first, second))
    old_exp = jnp.where(visible, jnp.exp(scores - top), 0.0)
    first_exp = jnp.exp(first - top)
    second_exp = jnp.where(later, jnp.exp(second - top), 0.0)
    total = jnp.sum(old_exp, axis=-1, keepdims=True) + first_exp + second_exp
    old_w = (old_exp / total).astype(BF16)
    first_w = (first_exp / total).astype(BF16).astype(F32)
    second_w = (second_exp / total).astype(BF16).astype(F32)
    mine = lax.broadcasted_iota(jnp.int32, (8, HEAD_DIM), 0) // 2 == row
    for slot in range(SLOTS):
        part = slice(slot * 8, slot * 8 + 8)
        result = jnp.dot(old_w[part], held[1, slot], preferred_element_type=F32)
        result = result + (
            first_w[part] * fresh[2, 0, slot : slot + 1]
            + second_w[part] * fresh[2, 1, slot : slot + 1]
        )
        att_scr[slot] = jnp.where(mine, result, 0.0)
    for target in range(ROWS):
        pair = [
            att_scr[slot_scr[(target * OLD + lane) * HEAD_DEV + i]] for i in range(HEAD_DEV)
        ]
        att_ref[target, : HEAD_DEV * 8] = jnp.concatenate(pair, axis=0).astype(BF16)
    for copy in copies:
        copy.wait()


def attend_and_pick(slot_map, lengths, cache, fresh):
    block = (2, HEAD_DEV, LEN, HEAD_DIM)
    return pl.pallas_call(
        attend_kernel,
        out_shape=(
            jax.ShapeDtypeStruct((ROWS, 96, HEAD_DIM), BF16),
            *[jax.ShapeDtypeStruct(block, BF16)] * ROWS,
        ),
        in_specs=[ANY] * 4,
        out_specs=(VMEM, *[ANY] * ROWS),
        scratch_shapes=[
            pltpu.SMEM(slot_map.shape, jnp.int32),
            pltpu.SMEM(lengths.shape, jnp.int32),
            pltpu.VMEM(fresh.shape, BF16),
            pltpu.VMEM((2, SLOTS, LEN, HEAD_DIM), BF16),
            pltpu.VMEM((SLOTS, 8, HEAD_DIM), F32),
            pltpu.SemaphoreType.DMA((5,)),
            pltpu.SemaphoreType.DMA((ROWS * HEAD_DEV * 2,)),
        ],
        cost_estimate=estimate(3.5),
        compiler_params=pltpu.CompilerParams(vmem_limit_bytes=FIRST_LIMIT),
        name="attend_and_pick",
    )(slot_map, lengths, cache, fresh)


def touch_kernel(weight_ref, out_ref):
    out_ref[...] = jnp.zeros_like(out_ref)


def touch(out_weight):
    return pl.pallas_call(
        touch_kernel,
        out_shape=jax.ShapeDtypeStruct((16, 128), BF16),
        in_specs=[ANY],
        out_specs=VMEM,
        cost_estimate=estimate(0.2),
        compiler_params=pltpu.CompilerParams(vmem_limit_bytes=VMEM_LIMIT),
        name="touch",
    )(out_weight)


def project_kernel(att_ref, weight_ref, *refs):
    out_ref = refs[-1]
    total = att_ref[0, : HEAD_DEV * 8].astype(F32)
    for row in range(1, ROWS):
        total = total + att_ref[row, : HEAD_DEV * 8].astype(F32)
    features = jnp.concatenate([total[:8], total[8:]], axis=1).astype(BF16)
    for chip in range(CHIPS):
        part = jnp.dot(
            features,
            weight_ref[:, chip * CHUNK : (chip + 1) * CHUNK],
            preferred_element_type=F32,
        )
        out_ref[chip] = part.astype(BF16)


def project(attended, out_weight, *arrived):
    return pl.pallas_call(
        project_kernel,
        out_shape=jax.ShapeDtypeStruct((CHIPS, 8, CHUNK), BF16),
        in_specs=[VMEM, VMEM] + [ANY] * len(arrived),
        out_specs=VMEM,
        cost_estimate=estimate(0.6),
        compiler_params=pltpu.CompilerParams(vmem_limit_bytes=VMEM_LIMIT),
        name="project",
    )(attended, out_weight, *arrived)


def widen_kernel(residual_ref, out_ref):
    core = lax.axis_index("head") % CORES
    own = jnp.concatenate([residual_ref[row].astype(F32) for row in range(ROWS)], axis=0)
    none = jnp.zeros_like(own)
    out_ref[...] = jnp.concatenate(
        [jnp.where(core == 0, own, none), jnp.where(core == 1, own, none)], axis=1
    )


def widen(residual):
    return pl.pallas_call(
        widen_kernel,
        out_shape=jax.ShapeDtypeStruct((8, CHUNK), F32),
        in_specs=[VMEM],
        out_specs=VMEM,
        cost_estimate=estimate(0.7),
        compiler_params=pltpu.CompilerParams(vmem_limit_bytes=VMEM_LIMIT),
        name="widen",
    )(residual)


def add_kernel(parts_ref, residual_ref, out_ref):
    total = parts_ref[0].astype(F32)
    for chip in range(1, CHIPS):
        total = total + parts_ref[chip].astype(F32)
    out_ref[...] = total + residual_ref[...]


def add_residual(parts, residual):
    return pl.pallas_call(
        add_kernel,
        out_shape=jax.ShapeDtypeStruct((8, CHUNK), F32),
        in_specs=[VMEM, VMEM],
        out_specs=VMEM,
        cost_estimate=estimate(0.2),
        compiler_params=pltpu.CompilerParams(vmem_limit_bytes=VMEM_LIMIT),
        name="add_residual",
    )(parts, residual)


def hidden_kernel(sums_ref, spread_ref):
    hidden = (sums_ref[0] + sums_ref[1]).astype(BF16)
    for chip in range(CHIPS):
        spread_ref[chip] = hidden


def round_hidden(sums):
    return pl.pallas_call(
        hidden_kernel,
        out_shape=jax.ShapeDtypeStruct((CHIPS, 8, CHUNK), BF16),
        in_specs=[VMEM],
        out_specs=VMEM,
        cost_estimate=estimate(0.2),
        compiler_params=pltpu.CompilerParams(vmem_limit_bytes=VMEM_LIMIT),
        name="round_hidden",
    )(sums)


def place(offsets, refs, cache_ref, sems):
    row = lax.axis_index("head") // OLD
    copies = []
    for offset, ref in zip(offsets, refs):
        source = (row + ROWS - offset) % ROWS
        for kind in range(2):
            copy = pltpu.make_async_copy(
                ref.at[kind], cache_ref.at[0, source, kind], sems.at[len(copies)]
            )
            copy.start()
            copies.append(copy)
    return copies


def norm_kernel(offsets, blocks_ref, gain_ref, bias_ref, *refs):
    *kv_refs, out_ref, hidden_ref, cache_ref, sems = refs
    copies = place(offsets, kv_refs, cache_ref, sems)
    me = lax.axis_index("head")
    own = blocks_ref[me // CORES].astype(F32)
    own = jnp.where(me % CORES == 0, own[:, :SHARE], own[:, SHARE:]).astype(BF16)
    for step in range(ROWS):
        hidden_ref[step] = own[2 * step : 2 * step + 2]
    total = blocks_ref[0].astype(F32)
    for chip in range(1, CHIPS):
        total = total + blocks_ref[chip].astype(F32)
    mean = jnp.sum(total, axis=-1, keepdims=True) / OUT
    spread = jnp.zeros((8, CHUNK), F32)
    for chip in range(CHIPS):
        spread = spread + (blocks_ref[chip].astype(F32) - mean) ** 2
    var = jnp.sum(spread, axis=-1, keepdims=True) / OUT
    scale = 1.0 / jnp.sqrt(var + 1e-05)
    tiles = CHUNK // 128
    for chip in range(CHIPS):
        values = (blocks_ref[chip].astype(F32) - mean) * scale
        for tile in range(tiles):
            at = chip * tiles + tile
            part = values[:, tile * 128 : (tile + 1) * 128]
            part = (part * gain_ref[at : at + 1] + bias_ref[at : at + 1]).astype(BF16)
            for step in range(ROWS):
                out_ref[step, :, at * 128 : (at + 1) * 128] = part[2 * step : 2 * step + 2]
    for copy in copies:
        copy.wait()


def normalize(blocks, gain, bias, offsets, kv):
    return pl.pallas_call(
        functools.partial(norm_kernel, offsets),
        out_shape=(
            jax.ShapeDtypeStruct((ROWS, 2, OUT), BF16),
            jax.ShapeDtypeStruct((ROWS, 2, SHARE), BF16),
            jax.ShapeDtypeStruct((1, ROWS) + kv[0].shape, BF16),
        ),
        in_specs=[VMEM] * (3 + len(kv)),
        out_specs=(VMEM, VMEM, HBM),
        scratch_shapes=[pltpu.SemaphoreType.DMA((2 * len(kv),))],
        cost_estimate=estimate(1.4),
        compiler_params=pltpu.CompilerParams(vmem_limit_bytes=VMEM_LIMIT),
        name="normalize",
    )(blocks, gain.reshape(OUT // 128, 128), bias.reshape(OUT // 128, 128), *kv)


def last_kernel(offset, block_ref, _, cache_ref, sems):
    for copy in place((offset,), (block_ref,), cache_ref, sems):
        copy.wait()


def place_last(offset, block, cache_new):
    return pl.pallas_call(
        functools.partial(last_kernel, offset),
        out_shape=jax.ShapeDtypeStruct(cache_new.shape, BF16),
        in_specs=[VMEM, HBM],
        out_specs=HBM,
        scratch_shapes=[pltpu.SemaphoreType.DMA((2,))],
        input_output_aliases={1: 0},
        cost_estimate=estimate(0.6),
        compiler_params=pltpu.CompilerParams(vmem_limit_bytes=VMEM_LIMIT),
        name="place_last",
    )(block, cache_new)


def exchange(blocks, groups):
    return lax.all_to_all(blocks, "head", 0, 0, axis_index_groups=groups, tiled=True)


def body(cache, fresh, slot_map, lengths, out_weight, residual, norm_gain, norm_bias):
    columns = [[row * OLD + lane for row in range(ROWS)] for lane in range(OLD)]
    sides = [[chip * CORES + core for chip in range(CHIPS)] for core in range(CORES)]
    pairs = [[chip * CORES + core for core in range(CORES)] for chip in range(CHIPS)]
    picked, *kv = attend_and_pick(slot_map, lengths, cache, fresh)
    first, inner = 1, (2, 3)

    def shifted(offset):
        pairs = [(i, (i + offset * OLD) % MEMBERS) for i in range(MEMBERS)]
        return lax.ppermute(kv[offset], "head", pairs)

    def region(run, *operands):
        def none(*operands):
            return jax.tree.map(lambda t: jnp.zeros(t.shape, t.dtype), jax.eval_shape(run, *operands))

        return lax.cond(lax.axis_index("head") < MEMBERS, run, none, *operands)

    def finish(total):
        sums = lax.all_gather(total, "head", axis_index_groups=pairs)
        return exchange(round_hidden(sums), sides)

    def middle(attended, weight, residual, gain, bias, *seen):
        parts = exchange(project(attended, weight, *seen), sides)
        moved = [shifted(offset) for offset in inner]
        blocks = region(finish, add_residual(parts, widen(residual)))
        return normalize(blocks, gain, bias, (0,) + inner, (kv[0], *moved))

    moved = shifted(first)
    attended = exchange(picked, columns)
    normed, hidden, cache_new = region(
        middle, attended, out_weight, residual, norm_gain, norm_bias, touch(out_weight)
    )
    return (place_last(first, moved, cache_new), hidden, normed)


def solution(mesh):
    in_specs = (
        P(("grp", "head"), None, None, None, None),
        P(("grp", "head"), None, None, None, None),
        P("grp"),
        P("grp"),
        P("head", None),
        P("grp", None, "head"),
        P(),
        P(),
    )
    out_specs = (
        P(("grp", "head"), None, None, None, None, None),
        P("grp", None, "head"),
        P("grp", None, None),
    )
    return jax.shard_map(body, mesh=mesh, in_specs=in_specs, out_specs=out_specs, check_vma=False)
```

```python
import functools
import math

import jax
import jax.numpy as jnp
from jax import lax
from jax.experimental import pallas as pl
from jax.experimental.pallas import tpu as pltpu
from jax.sharding import PartitionSpec as P

ROWS = 4
HEAD_DEV = 2
HEAD_DIM = 128
SLOTS = 8
LEN = 128
OUT = 6144
MEMBERS = 32
CORES = 2
CHIPS = MEMBERS // CORES
OLD = MEMBERS // ROWS
SHARE = OUT // MEMBERS
CHUNK = OUT // CHIPS
SIDE = 4
RANK = [chip % SIDE * SIDE + chip // SIDE for chip in range(CHIPS)]
BLOCK = 2 * HEAD_DEV * LEN
FEW = HEAD_DEV * 8
EARLY = 64
LATE = BLOCK - EARLY
F32 = jnp.float32
BF16 = jnp.bfloat16
FIRST_LIMIT = 56 * 2**20
VMEM_LIMIT = 8 * 2**20
SMEM = pl.BlockSpec(memory_space=pltpu.SMEM)
VMEM = pl.BlockSpec(memory_space=pltpu.VMEM)
ANY = pl.BlockSpec(memory_space=pl.ANY)
HBM = pl.BlockSpec(memory_space=pltpu.HBM)


def estimate(microseconds):
    return pl.CostEstimate(
        flops=0, transcendentals=0, bytes_accessed=int(microseconds * 3.69e6)
    )


def attend_kernel(
    slot_hbm, len_hbm, cache_ref, fresh_hbm, att_ref, kv0, kv1, kv2, kv3,
    slot_scr, len_scr, fresh_scr, held, att_scr, in_sems, sems,
):
    me = lax.axis_index("head")
    row = me // OLD
    lane = me % OLD
    loads = []
    for source, target in (
        (cache_ref.at[0, 0], held.at[0]),
        (fresh_hbm, fresh_scr),
        (slot_hbm, slot_scr),
        (len_hbm, len_scr),
        (cache_ref.at[0, 1], held.at[1]),
    ):
        load = pltpu.make_async_copy(source, target, in_sems.at[len(loads)])
        load.start()
        loads.append(load)
    copies = []

    def pick(kind):
        for offset, kv_ref in ((1, kv1), (2, kv2), (3, kv3), (0, kv0)):
            target = (row + offset) % ROWS
            for i in range(HEAD_DEV):
                slot = slot_scr[(target * OLD + lane) * HEAD_DEV + i]
                at = (kind * HEAD_DEV + i) * LEN
                rows = min(LEN, LATE - at)
                if rows <= 0:
                    continue
                copy = pltpu.make_async_copy(
                    held.at[kind, slot, pl.ds(0, rows)],
                    kv_ref.at[pl.ds(at, rows)],
                    sems.at[len(copies)],
                )
                copy.start()
                copies.append(copy)

    scale = 1.0 / math.sqrt(HEAD_DIM)
    query_rows, old_scores, new_first, new_second = [], [], [], []
    odd = lax.broadcasted_iota(jnp.int32, (8, HEAD_DIM), 0) % 2 == 1
    loads[1].wait()
    fresh = fresh_scr[0].astype(F32)
    for slot in range(SLOTS):
        query = jnp.where(
            odd,
            jnp.broadcast_to(fresh[0, 1, slot : slot + 1], (8, HEAD_DIM)),
            jnp.broadcast_to(fresh[0, 0, slot : slot + 1], (8, HEAD_DIM)),
        )
        query_rows.append(query.astype(BF16))
        new_first.append(jnp.sum(query * fresh[1, 0, slot : slot + 1], axis=-1, keepdims=True))
        new_second.append(jnp.sum(query * fresh[1, 1, slot : slot + 1], axis=-1, keepdims=True))
    loads[0].wait()
    loads[2].wait()
    pick(0)
    for slot in range(SLOTS):
        old_scores.append(
            lax.dot_general(
                query_rows[slot],
                held[0, slot],
                (((1,), (1,)), ((), ())),
                preferred_element_type=F32,
            )
        )
    loads[4].wait()
    pick(1)
    shape = (SLOTS * 8, LEN)
    scores = jnp.concatenate(old_scores, axis=0) * scale
    first = jnp.concatenate(new_first, axis=0) * scale
    second = jnp.concatenate(new_second, axis=0) * scale
    loads[3].wait()
    visible = lax.broadcasted_iota(jnp.int32, shape, 1) < len_scr[row]
    later = lax.broadcasted_iota(jnp.int32, (SLOTS * 8, 1), 0) % 2 == 1
    scores = jnp.where(visible, scores, -1e30)
    second = jnp.where(later, second, -1e30)
    top = jnp.maximum(jnp.max(scores, axis=-1, keepdims=True), jnp.maximum(first, second))
    old_exp = jnp.where(visible, jnp.exp(scores - top), 0.0)
    first_exp = jnp.exp(first - top)
    second_exp = jnp.where(later, jnp.exp(second - top), 0.0)
    total = jnp.sum(old_exp, axis=-1, keepdims=True) + first_exp + second_exp
    old_w = (old_exp / total).astype(BF16)
    first_w = (first_exp / total).astype(BF16).astype(F32)
    second_w = (second_exp / total).astype(BF16).astype(F32)
    mine = lax.broadcasted_iota(jnp.int32, (8, HEAD_DIM), 0) // 2 == row
    for slot in range(SLOTS):
        part = slice(slot * 8, slot * 8 + 8)
        result = jnp.dot(old_w[part], held[1, slot], preferred_element_type=F32)
        result = result + (
            first_w[part] * fresh[2, 0, slot : slot + 1]
            + second_w[part] * fresh[2, 1, slot : slot + 1]
        )
        att_scr[slot] = jnp.where(mine, result, 0.0)
    for target in range(ROWS):
        pair = [
            att_scr[slot_scr[(target * OLD + lane) * HEAD_DEV + i]] for i in range(HEAD_DEV)
        ]
        att_ref[target, :FEW] = jnp.concatenate(pair, axis=0).astype(BF16)
        slot = slot_scr[(target * OLD + lane) * HEAD_DEV + HEAD_DEV - 1]
        att_ref[target, FEW:] = held[1, slot, LEN - EARLY :]
    for copy in copies:
        copy.wait()


def attend_and_pick(slot_map, lengths, cache, fresh):
    return pl.pallas_call(
        attend_kernel,
        out_shape=(
            jax.ShapeDtypeStruct((ROWS, FEW + EARLY, HEAD_DIM), BF16),
            *[jax.ShapeDtypeStruct((LATE, HEAD_DIM), BF16)] * ROWS,
        ),
        in_specs=[ANY] * 4,
        out_specs=(VMEM, *[ANY] * ROWS),
        scratch_shapes=[
            pltpu.SMEM(slot_map.shape, jnp.int32),
            pltpu.SMEM(lengths.shape, jnp.int32),
            pltpu.VMEM(fresh.shape, BF16),
            pltpu.VMEM((2, SLOTS, LEN, HEAD_DIM), BF16),
            pltpu.VMEM((SLOTS, 8, HEAD_DIM), F32),
            pltpu.SemaphoreType.DMA((5,)),
            pltpu.SemaphoreType.DMA((ROWS * HEAD_DEV * 2,)),
        ],
        cost_estimate=estimate(3.5),
        compiler_params=pltpu.CompilerParams(vmem_limit_bytes=FIRST_LIMIT),
        name="attend_and_pick",
    )(slot_map, lengths, cache, fresh)


def touch_kernel(weight_ref, out_ref):
    out_ref[...] = jnp.zeros_like(out_ref)


def touch(out_weight):
    return pl.pallas_call(
        touch_kernel,
        out_shape=jax.ShapeDtypeStruct((16, 128), BF16),
        in_specs=[ANY],
        out_specs=VMEM,
        cost_estimate=estimate(0.2),
        compiler_params=pltpu.CompilerParams(vmem_limit_bytes=VMEM_LIMIT),
        name="touch",
    )(out_weight)


def project_kernel(att_ref, weight_ref, *refs):
    out_ref = refs[-1]
    total = att_ref[0, :FEW].astype(F32)
    for row in range(1, ROWS):
        total = total + att_ref[row, :FEW].astype(F32)
    features = jnp.concatenate([total[:8], total[8:]], axis=1).astype(BF16)
    for chip in range(CHIPS):
        part = jnp.dot(
            features,
            weight_ref[:, chip * CHUNK : (chip + 1) * CHUNK],
            preferred_element_type=F32,
        )
        out_ref[RANK[chip]] = part.astype(BF16)


def project(attended, out_weight, *arrived):
    return pl.pallas_call(
        project_kernel,
        out_shape=jax.ShapeDtypeStruct((CHIPS, 8, CHUNK), BF16),
        in_specs=[VMEM, VMEM] + [ANY] * len(arrived),
        out_specs=VMEM,
        cost_estimate=estimate(0.6),
        compiler_params=pltpu.CompilerParams(vmem_limit_bytes=VMEM_LIMIT),
        name="project",
    )(attended, out_weight, *arrived)


def widen_kernel(residual_ref, out_ref):
    core = lax.axis_index("head") % CORES
    own = jnp.concatenate([residual_ref[row].astype(F32) for row in range(ROWS)], axis=0)
    none = jnp.zeros_like(own)
    out_ref[...] = jnp.concatenate(
        [jnp.where(core == 0, own, none), jnp.where(core == 1, own, none)], axis=1
    )


def widen(residual):
    return pl.pallas_call(
        widen_kernel,
        out_shape=jax.ShapeDtypeStruct((8, CHUNK), F32),
        in_specs=[VMEM],
        out_specs=VMEM,
        cost_estimate=estimate(0.7),
        compiler_params=pltpu.CompilerParams(vmem_limit_bytes=VMEM_LIMIT),
        name="widen",
    )(residual)


def add_kernel(parts_ref, residual_ref, out_ref):
    total = parts_ref[0].astype(F32)
    for chip in range(1, CHIPS):
        total = total + parts_ref[chip].astype(F32)
    out_ref[...] = total + residual_ref[...]


def add_residual(parts, residual):
    return pl.pallas_call(
        add_kernel,
        out_shape=jax.ShapeDtypeStruct((8, CHUNK), F32),
        in_specs=[VMEM, VMEM],
        out_specs=VMEM,
        cost_estimate=estimate(0.2),
        compiler_params=pltpu.CompilerParams(vmem_limit_bytes=VMEM_LIMIT),
        name="add_residual",
    )(parts, residual)


def hidden_kernel(sums_ref, spread_ref):
    hidden = (sums_ref[0] + sums_ref[1]).astype(BF16)
    for chip in range(CHIPS):
        spread_ref[chip] = hidden


def round_hidden(sums):
    return pl.pallas_call(
        hidden_kernel,
        out_shape=jax.ShapeDtypeStruct((CHIPS, 8, CHUNK), BF16),
        in_specs=[VMEM],
        out_specs=VMEM,
        cost_estimate=estimate(0.2),
        compiler_params=pltpu.CompilerParams(vmem_limit_bytes=VMEM_LIMIT),
        name="round_hidden",
    )(sums)


def place(offsets, refs, cache_ref, sems):
    row = lax.axis_index("head") // OLD
    copies = []
    for offset, ref in zip(offsets, refs):
        source = (row + ROWS - offset) % ROWS
        for part in (pl.ds(0, BLOCK // 2), pl.ds(BLOCK // 2, LATE - BLOCK // 2)):
            copy = pltpu.make_async_copy(
                ref.at[part], cache_ref.at[0, source, part], sems.at[len(copies)]
            )
            copy.start()
            copies.append(copy)
    return copies


def norm_kernel(offsets, blocks_ref, gain_ref, bias_ref, early_ref, *refs):
    *kv_refs, out_ref, hidden_ref, cache_ref, sems = refs
    copies = place(offsets, kv_refs, cache_ref, sems)
    for row in range(ROWS):
        copy = pltpu.make_async_copy(
            early_ref.at[row, pl.ds(FEW, EARLY)],
            cache_ref.at[0, row, pl.ds(LATE, EARLY)],
            sems.at[len(copies)],
        )
        copy.start()
        copies.append(copy)
    me = lax.axis_index("head")
    chip = me // CORES
    own = blocks_ref[chip % SIDE * SIDE + chip // SIDE].astype(F32)
    own = jnp.where(me % CORES == 0, own[:, :SHARE], own[:, SHARE:]).astype(BF16)
    for step in range(ROWS):
        hidden_ref[step] = own[2 * step : 2 * step + 2]
    total = blocks_ref[0].astype(F32)
    for chip in range(1, CHIPS):
        total = total + blocks_ref[chip].astype(F32)
    mean = jnp.sum(total, axis=-1, keepdims=True) / OUT
    spread = jnp.zeros((8, CHUNK), F32)
    for chip in range(CHIPS):
        spread = spread + (blocks_ref[chip].astype(F32) - mean) ** 2
    var = jnp.sum(spread, axis=-1, keepdims=True) / OUT
    scale = 1.0 / jnp.sqrt(var + 1e-05)
    tiles = CHUNK // 128
    for chip in range(CHIPS):
        values = (blocks_ref[RANK[chip]].astype(F32) - mean) * scale
        for tile in range(tiles):
            at = chip * tiles + tile
            part = values[:, tile * 128 : (tile + 1) * 128]
            part = (part * gain_ref[at : at + 1] + bias_ref[at : at + 1]).astype(BF16)
            for step in range(ROWS):
                out_ref[step, :, at * 128 : (at + 1) * 128] = part[2 * step : 2 * step + 2]
    for copy in copies:
        copy.wait()


def normalize(blocks, gain, bias, early, offsets, kv):
    return pl.pallas_call(
        functools.partial(norm_kernel, offsets),
        out_shape=(
            jax.ShapeDtypeStruct((ROWS, 2, OUT), BF16),
            jax.ShapeDtypeStruct((ROWS, 2, SHARE), BF16),
            jax.ShapeDtypeStruct((1, ROWS, BLOCK, HEAD_DIM), BF16),
        ),
        in_specs=[VMEM] * (4 + len(kv)),
        out_specs=(VMEM, VMEM, HBM),
        scratch_shapes=[pltpu.SemaphoreType.DMA((2 * len(kv) + ROWS,))],
        cost_estimate=estimate(1.4),
        compiler_params=pltpu.CompilerParams(vmem_limit_bytes=VMEM_LIMIT),
        name="normalize",
    )(
        blocks,
        gain.reshape(OUT // 128, 128),
        bias.reshape(OUT // 128, 128),
        early,
        *kv,
    )


def last_kernel(offset, block_ref, _, cache_ref, sems):
    for copy in place((offset,), (block_ref,), cache_ref, sems):
        copy.wait()


def place_last(offset, block, cache_new):
    return pl.pallas_call(
        functools.partial(last_kernel, offset),
        out_shape=jax.ShapeDtypeStruct(cache_new.shape, BF16),
        in_specs=[VMEM, HBM],
        out_specs=HBM,
        scratch_shapes=[pltpu.SemaphoreType.DMA((2,))],
        input_output_aliases={1: 0},
        cost_estimate=estimate(0.6),
        compiler_params=pltpu.CompilerParams(vmem_limit_bytes=VMEM_LIMIT),
        name="place_last",
    )(block, cache_new)


def exchange(blocks, groups):
    return lax.all_to_all(blocks, "head", 0, 0, axis_index_groups=groups, tiled=True)


def body(cache, fresh, slot_map, lengths, out_weight, residual, norm_gain, norm_bias):
    columns = [[row * OLD + lane for row in range(ROWS)] for lane in range(OLD)]
    sides = [[RANK[chip] * CORES + core for chip in range(CHIPS)] for core in range(CORES)]
    pairs = [[chip * CORES + core for core in range(CORES)] for chip in range(CHIPS)]
    picked, *kv = attend_and_pick(slot_map, lengths, cache, fresh)
    first, inner = 1, (2, 3)

    def shifted(offset):
        pairs = [(i, (i + offset * OLD) % MEMBERS) for i in range(MEMBERS)]
        return lax.ppermute(kv[offset], "head", pairs)

    def region(run, *operands):
        def none(*operands):
            return jax.tree.map(lambda t: jnp.zeros(t.shape, t.dtype), jax.eval_shape(run, *operands))

        return lax.cond(lax.axis_index("head") < MEMBERS, run, none, *operands)

    def finish(total):
        sums = lax.all_gather(total, "head", axis_index_groups=pairs)
        return exchange(round_hidden(sums), sides)

    def middle(attended, weight, residual, gain, bias, *seen):
        parts = exchange(project(attended, weight, *seen), sides)
        moved = [shifted(offset) for offset in inner]
        blocks = region(finish, add_residual(parts, widen(residual)))
        return normalize(blocks, gain, bias, attended, (0,) + inner, (kv[0], *moved))

    moved = shifted(first)
    attended = exchange(picked, columns)
    normed, hidden, cache_new = region(
        middle, attended, out_weight, residual, norm_gain, norm_bias, touch(out_weight)
    )
    cache_new = place_last(first, moved, cache_new)
    return (cache_new.reshape(1, ROWS, 2, HEAD_DEV, LEN, HEAD_DIM), hidden, normed)


def solution(mesh):
    in_specs = (
        P(("grp", "head"), None, None, None, None),
        P(("grp", "head"), None, None, None, None),
        P("grp"),
        P("grp"),
        P("head", None),
        P("grp", None, "head"),
        P(),
        P(),
    )
    out_specs = (
        P(("grp", "head"), None, None, None, None, None),
        P("grp", None, "head"),
        P("grp", None, None),
    )
    return jax.shard_map(body, mesh=mesh, in_specs=in_specs, out_specs=out_specs, check_vma=False)
```

```python
import functools
import math

import jax
import jax.numpy as jnp
from jax import lax
from jax.experimental import pallas as pl
from jax.experimental.pallas import tpu as pltpu
from jax.sharding import PartitionSpec as P

ROWS = 4
HEAD_DEV = 2
HEAD_DIM = 128
SLOTS = 8
LEN = 128
OUT = 6144
MEMBERS = 32
CORES = 2
CHIPS = MEMBERS // CORES
OLD = MEMBERS // ROWS
SHARE = OUT // MEMBERS
CHUNK = OUT // CHIPS
SUM_ORDER = [0, 1, 2, 3, 4, 5, 6, 7, 8, 9, 10, 11, 12, 13, 14, 15]
ROW_ORDER = [2, 6, 10, 14, 3, 7, 11, 15, 0, 4, 8, 12, 1, 5, 9, 13]
SUM_RANK = [SUM_ORDER.index(chip) for chip in range(CHIPS)]
ROW_RANK = [ROW_ORDER.index(chip) for chip in range(CHIPS)]
BLOCK = 2 * HEAD_DEV * LEN
FEW = HEAD_DEV * 8
EARLY = 64
LATE = BLOCK - EARLY
F32 = jnp.float32
BF16 = jnp.bfloat16
FIRST_LIMIT = 56 * 2**20
VMEM_LIMIT = 8 * 2**20
SMEM = pl.BlockSpec(memory_space=pltpu.SMEM)
VMEM = pl.BlockSpec(memory_space=pltpu.VMEM)
ANY = pl.BlockSpec(memory_space=pl.ANY)
HBM = pl.BlockSpec(memory_space=pltpu.HBM)


def estimate(microseconds):
    return pl.CostEstimate(
        flops=0, transcendentals=0, bytes_accessed=int(microseconds * 3.69e6)
    )


def attend_kernel(
    slot_hbm, len_hbm, cache_ref, fresh_hbm, att_ref, kv0, kv1, kv2, kv3,
    slot_scr, len_scr, fresh_scr, held, att_scr, in_sems, sems,
):
    me = lax.axis_index("head")
    row = me // OLD
    lane = me % OLD
    loads = []
    for source, target in (
        (cache_ref.at[0, 0], held.at[0]),
        (fresh_hbm, fresh_scr),
        (slot_hbm, slot_scr),
        (len_hbm, len_scr),
        (cache_ref.at[0, 1], held.at[1]),
    ):
        load = pltpu.make_async_copy(source, target, in_sems.at[len(loads)])
        load.start()
        loads.append(load)
    copies = []

    def pick(kind):
        for offset, kv_ref in ((1, kv1), (2, kv2), (3, kv3), (0, kv0)):
            target = (row + offset) % ROWS
            for i in range(HEAD_DEV):
                slot = slot_scr[(target * OLD + lane) * HEAD_DEV + i]
                at = (kind * HEAD_DEV + i) * LEN
                rows = min(LEN, LATE - at)
                if rows <= 0:
                    continue
                copy = pltpu.make_async_copy(
                    held.at[kind, slot, pl.ds(0, rows)],
                    kv_ref.at[pl.ds(at, rows)],
                    sems.at[len(copies)],
                )
                copy.start()
                copies.append(copy)

    scale = 1.0 / math.sqrt(HEAD_DIM)
    query_rows, old_scores, new_first, new_second = [], [], [], []
    odd = lax.broadcasted_iota(jnp.int32, (8, HEAD_DIM), 0) % 2 == 1
    loads[1].wait()
    fresh = fresh_scr[0].astype(F32)
    for slot in range(SLOTS):
        query = jnp.where(
            odd,
            jnp.broadcast_to(fresh[0, 1, slot : slot + 1], (8, HEAD_DIM)),
            jnp.broadcast_to(fresh[0, 0, slot : slot + 1], (8, HEAD_DIM)),
        )
        query_rows.append(query.astype(BF16))
        new_first.append(jnp.sum(query * fresh[1, 0, slot : slot + 1], axis=-1, keepdims=True))
        new_second.append(jnp.sum(query * fresh[1, 1, slot : slot + 1], axis=-1, keepdims=True))
    loads[0].wait()
    loads[2].wait()
    pick(0)
    for slot in range(SLOTS):
        old_scores.append(
            lax.dot_general(
                query_rows[slot],
                held[0, slot],
                (((1,), (1,)), ((), ())),
                preferred_element_type=F32,
            )
        )
    loads[4].wait()
    pick(1)
    shape = (SLOTS * 8, LEN)
    scores = jnp.concatenate(old_scores, axis=0) * scale
    first = jnp.concatenate(new_first, axis=0) * scale
    second = jnp.concatenate(new_second, axis=0) * scale
    loads[3].wait()
    visible = lax.broadcasted_iota(jnp.int32, shape, 1) < len_scr[row]
    later = lax.broadcasted_iota(jnp.int32, (SLOTS * 8, 1), 0) % 2 == 1
    scores = jnp.where(visible, scores, -1e30)
    second = jnp.where(later, second, -1e30)
    top = jnp.maximum(jnp.max(scores, axis=-1, keepdims=True), jnp.maximum(first, second))
    old_exp = jnp.where(visible, jnp.exp(scores - top), 0.0)
    first_exp = jnp.exp(first - top)
    second_exp = jnp.where(later, jnp.exp(second - top), 0.0)
    total = jnp.sum(old_exp, axis=-1, keepdims=True) + first_exp + second_exp
    old_w = (old_exp / total).astype(BF16)
    first_w = (first_exp / total).astype(BF16).astype(F32)
    second_w = (second_exp / total).astype(BF16).astype(F32)
    mine = lax.broadcasted_iota(jnp.int32, (8, HEAD_DIM), 0) // 2 == row
    for slot in range(SLOTS):
        part = slice(slot * 8, slot * 8 + 8)
        result = jnp.dot(old_w[part], held[1, slot], preferred_element_type=F32)
        result = result + (
            first_w[part] * fresh[2, 0, slot : slot + 1]
            + second_w[part] * fresh[2, 1, slot : slot + 1]
        )
        att_scr[slot] = jnp.where(mine, result, 0.0)
    for target in range(ROWS):
        pair = [
            att_scr[slot_scr[(target * OLD + lane) * HEAD_DEV + i]] for i in range(HEAD_DEV)
        ]
        att_ref[target, :FEW] = jnp.concatenate(pair, axis=0).astype(BF16)
        slot = slot_scr[(target * OLD + lane) * HEAD_DEV + HEAD_DEV - 1]
        att_ref[target, FEW:] = held[1, slot, LEN - EARLY :]
    for copy in copies:
        copy.wait()


def attend_and_pick(slot_map, lengths, cache, fresh):
    return pl.pallas_call(
        attend_kernel,
        out_shape=(
            jax.ShapeDtypeStruct((ROWS, FEW + EARLY, HEAD_DIM), BF16),
            *[jax.ShapeDtypeStruct((LATE, HEAD_DIM), BF16)] * ROWS,
        ),
        in_specs=[ANY] * 4,
        out_specs=(VMEM, *[ANY] * ROWS),
        scratch_shapes=[
            pltpu.SMEM(slot_map.shape, jnp.int32),
            pltpu.SMEM(lengths.shape, jnp.int32),
            pltpu.VMEM(fresh.shape, BF16),
            pltpu.VMEM((2, SLOTS, LEN, HEAD_DIM), BF16),
            pltpu.VMEM((SLOTS, 8, HEAD_DIM), F32),
            pltpu.SemaphoreType.DMA((5,)),
            pltpu.SemaphoreType.DMA((ROWS * HEAD_DEV * 2,)),
        ],
        cost_estimate=estimate(3.5),
        compiler_params=pltpu.CompilerParams(vmem_limit_bytes=FIRST_LIMIT),
        name="attend_and_pick",
    )(slot_map, lengths, cache, fresh)


def touch_kernel(weight_ref, out_ref):
    out_ref[...] = jnp.zeros_like(out_ref)


def touch(out_weight):
    return pl.pallas_call(
        touch_kernel,
        out_shape=jax.ShapeDtypeStruct((16, 128), BF16),
        in_specs=[ANY],
        out_specs=VMEM,
        cost_estimate=estimate(0.2),
        compiler_params=pltpu.CompilerParams(vmem_limit_bytes=VMEM_LIMIT),
        name="touch",
    )(out_weight)


def project_kernel(att_ref, weight_ref, *refs):
    out_ref = refs[-1]
    total = att_ref[0, :FEW].astype(F32)
    for row in range(1, ROWS):
        total = total + att_ref[row, :FEW].astype(F32)
    features = jnp.concatenate([total[:8], total[8:]], axis=1).astype(BF16)
    for chip in range(CHIPS):
        part = jnp.dot(
            features,
            weight_ref[:, chip * CHUNK : (chip + 1) * CHUNK],
            preferred_element_type=F32,
        )
        out_ref[SUM_RANK[chip]] = part.astype(BF16)


def project(attended, out_weight, *arrived):
    return pl.pallas_call(
        project_kernel,
        out_shape=jax.ShapeDtypeStruct((CHIPS, 8, CHUNK), BF16),
        in_specs=[VMEM, VMEM] + [ANY] * len(arrived),
        out_specs=VMEM,
        cost_estimate=estimate(0.6),
        compiler_params=pltpu.CompilerParams(vmem_limit_bytes=VMEM_LIMIT),
        name="project",
    )(attended, out_weight, *arrived)


def widen_kernel(residual_ref, out_ref):
    core = lax.axis_index("head") % CORES
    own = jnp.concatenate([residual_ref[row].astype(F32) for row in range(ROWS)], axis=0)
    none = jnp.zeros_like(own)
    out_ref[...] = jnp.concatenate(
        [jnp.where(core == 0, own, none), jnp.where(core == 1, own, none)], axis=1
    )


def widen(residual):
    return pl.pallas_call(
        widen_kernel,
        out_shape=jax.ShapeDtypeStruct((8, CHUNK), F32),
        in_specs=[VMEM],
        out_specs=VMEM,
        cost_estimate=estimate(0.7),
        compiler_params=pltpu.CompilerParams(vmem_limit_bytes=VMEM_LIMIT),
        name="widen",
    )(residual)


def add_kernel(parts_ref, residual_ref, out_ref):
    total = parts_ref[0].astype(F32)
    for chip in range(1, CHIPS):
        total = total + parts_ref[chip].astype(F32)
    out_ref[...] = total + residual_ref[...]


def add_residual(parts, residual):
    return pl.pallas_call(
        add_kernel,
        out_shape=jax.ShapeDtypeStruct((8, CHUNK), F32),
        in_specs=[VMEM, VMEM],
        out_specs=VMEM,
        cost_estimate=estimate(0.2),
        compiler_params=pltpu.CompilerParams(vmem_limit_bytes=VMEM_LIMIT),
        name="add_residual",
    )(parts, residual)


def hidden_kernel(sums_ref, spread_ref):
    hidden = (sums_ref[0] + sums_ref[1]).astype(BF16)
    for chip in range(CHIPS):
        spread_ref[chip] = hidden


def round_hidden(sums):
    return pl.pallas_call(
        hidden_kernel,
        out_shape=jax.ShapeDtypeStruct((CHIPS, 8, CHUNK), BF16),
        in_specs=[VMEM],
        out_specs=VMEM,
        cost_estimate=estimate(0.2),
        compiler_params=pltpu.CompilerParams(vmem_limit_bytes=VMEM_LIMIT),
        name="round_hidden",
    )(sums)


def place(offsets, refs, cache_ref, sems):
    row = lax.axis_index("head") // OLD
    copies = []
    for offset, ref in zip(offsets, refs):
        source = (row + ROWS - offset) % ROWS
        for part in (pl.ds(0, BLOCK // 2), pl.ds(BLOCK // 2, LATE - BLOCK // 2)):
            copy = pltpu.make_async_copy(
                ref.at[part], cache_ref.at[0, source, part], sems.at[len(copies)]
            )
            copy.start()
            copies.append(copy)
    return copies


def norm_kernel(offsets, blocks_ref, gain_ref, bias_ref, early_ref, *refs):
    *kv_refs, out_ref, hidden_ref, cache_ref, sems = refs
    copies = place(offsets, kv_refs, cache_ref, sems)
    for row in range(ROWS):
        copy = pltpu.make_async_copy(
            early_ref.at[row, pl.ds(FEW, EARLY)],
            cache_ref.at[0, row, pl.ds(LATE, EARLY)],
            sems.at[len(copies)],
        )
        copy.start()
        copies.append(copy)
    me = lax.axis_index("head")
    chip = me // CORES
    own = jnp.zeros((8, CHUNK), F32)
    for one in range(CHIPS):
        own = jnp.where(chip == one, blocks_ref[ROW_RANK[one]].astype(F32), own)
    own = jnp.where(me % CORES == 0, own[:, :SHARE], own[:, SHARE:]).astype(BF16)
    for step in range(ROWS):
        hidden_ref[step] = own[2 * step : 2 * step + 2]
    total = blocks_ref[0].astype(F32)
    for chip in range(1, CHIPS):
        total = total + blocks_ref[chip].astype(F32)
    mean = jnp.sum(total, axis=-1, keepdims=True) / OUT
    spread = jnp.zeros((8, CHUNK), F32)
    for chip in range(CHIPS):
        spread = spread + (blocks_ref[chip].astype(F32) - mean) ** 2
    var = jnp.sum(spread, axis=-1, keepdims=True) / OUT
    scale = 1.0 / jnp.sqrt(var + 1e-05)
    tiles = CHUNK // 128
    for chip in range(CHIPS):
        values = (blocks_ref[ROW_RANK[chip]].astype(F32) - mean) * scale
        for tile in range(tiles):
            at = chip * tiles + tile
            part = values[:, tile * 128 : (tile + 1) * 128]
            part = (part * gain_ref[at : at + 1] + bias_ref[at : at + 1]).astype(BF16)
            for step in range(ROWS):
                out_ref[step, :, at * 128 : (at + 1) * 128] = part[2 * step : 2 * step + 2]
    for copy in copies:
        copy.wait()


def normalize(blocks, gain, bias, early, offsets, kv):
    return pl.pallas_call(
        functools.partial(norm_kernel, offsets),
        out_shape=(
            jax.ShapeDtypeStruct((ROWS, 2, OUT), BF16),
            jax.ShapeDtypeStruct((ROWS, 2, SHARE), BF16),
            jax.ShapeDtypeStruct((1, ROWS, BLOCK, HEAD_DIM), BF16),
        ),
        in_specs=[VMEM] * (4 + len(kv)),
        out_specs=(VMEM, VMEM, HBM),
        scratch_shapes=[pltpu.SemaphoreType.DMA((2 * len(kv) + ROWS,))],
        cost_estimate=estimate(1.4),
        compiler_params=pltpu.CompilerParams(vmem_limit_bytes=VMEM_LIMIT),
        name="normalize",
    )(
        blocks,
        gain.reshape(OUT // 128, 128),
        bias.reshape(OUT // 128, 128),
        early,
        *kv,
    )


def last_kernel(offset, block_ref, _, cache_ref, sems):
    for copy in place((offset,), (block_ref,), cache_ref, sems):
        copy.wait()


def place_last(offset, block, cache_new):
    return pl.pallas_call(
        functools.partial(last_kernel, offset),
        out_shape=jax.ShapeDtypeStruct(cache_new.shape, BF16),
        in_specs=[VMEM, HBM],
        out_specs=HBM,
        scratch_shapes=[pltpu.SemaphoreType.DMA((2,))],
        input_output_aliases={1: 0},
        cost_estimate=estimate(0.6),
        compiler_params=pltpu.CompilerParams(vmem_limit_bytes=VMEM_LIMIT),
        name="place_last",
    )(block, cache_new)


def exchange(blocks, groups):
    return lax.all_to_all(blocks, "head", 0, 0, axis_index_groups=groups, tiled=True)


def body(cache, fresh, slot_map, lengths, out_weight, residual, norm_gain, norm_bias):
    columns = [[row * OLD + lane for row in range(ROWS)] for lane in range(OLD)]
    sum_sides = [[chip * CORES + core for chip in SUM_ORDER] for core in range(CORES)]
    row_sides = [[chip * CORES + core for chip in ROW_ORDER] for core in range(CORES)]
    pairs = [[chip * CORES + core for core in range(CORES)] for chip in range(CHIPS)]
    picked, *kv = attend_and_pick(slot_map, lengths, cache, fresh)
    first, inner = 1, (2, 3)

    def shifted(offset):
        pairs = [(i, (i + offset * OLD) % MEMBERS) for i in range(MEMBERS)]
        return lax.ppermute(kv[offset], "head", pairs)

    def region(run, *operands):
        def none(*operands):
            return jax.tree.map(lambda t: jnp.zeros(t.shape, t.dtype), jax.eval_shape(run, *operands))

        return lax.cond(lax.axis_index("head") < MEMBERS, run, none, *operands)

    def finish(total):
        sums = lax.all_gather(total, "head", axis_index_groups=pairs)
        return exchange(round_hidden(sums), row_sides)

    def middle(attended, weight, residual, gain, bias, *seen):
        parts = exchange(project(attended, weight, *seen), sum_sides)
        moved = [shifted(offset) for offset in inner]
        blocks = region(finish, add_residual(parts, widen(residual)))
        return normalize(blocks, gain, bias, attended, (0,) + inner, (kv[0], *moved))

    moved = shifted(first)
    attended = exchange(picked, columns)
    normed, hidden, cache_new = region(
        middle, attended, out_weight, residual, norm_gain, norm_bias, touch(out_weight)
    )
    cache_new = place_last(first, moved, cache_new)
    return (cache_new.reshape(1, ROWS, 2, HEAD_DEV, LEN, HEAD_DIM), hidden, normed)


def solution(mesh):
    in_specs = (
        P(("grp", "head"), None, None, None, None),
        P(("grp", "head"), None, None, None, None),
        P("grp"),
        P("grp"),
        P("head", None),
        P("grp", None, "head"),
        P(),
        P(),
    )
    out_specs = (
        P(("grp", "head"), None, None, None, None, None),
        P("grp", None, "head"),
        P("grp", None, None),
    )
    return jax.shard_map(body, mesh=mesh, in_specs=in_specs, out_specs=out_specs, check_vma=False)
```

```python
import functools
import math

import jax
import jax.numpy as jnp
from jax import lax
from jax.experimental import pallas as pl
from jax.experimental.pallas import tpu as pltpu
from jax.sharding import PartitionSpec as P

ROWS = 4
HEAD_DEV = 2
HEAD_DIM = 128
SLOTS = 8
LEN = 128
OUT = 6144
MEMBERS = 32
CORES = 2
CHIPS = MEMBERS // CORES
OLD = MEMBERS // ROWS
SHARE = OUT // MEMBERS
CHUNK = OUT // CHIPS
LINE_ORDER = [1, 2, 3, 0]
LINE_RANK = [LINE_ORDER.index(row) for row in range(ROWS)]
SUM_ORDER = [0, 1, 2, 3, 4, 5, 6, 7, 8, 9, 10, 11, 12, 13, 14, 15]
ROW_ORDER = [2, 6, 10, 14, 3, 7, 11, 15, 0, 4, 8, 12, 1, 5, 9, 13]
SUM_RANK = [SUM_ORDER.index(chip) for chip in range(CHIPS)]
ROW_RANK = [ROW_ORDER.index(chip) for chip in range(CHIPS)]
BLOCK = 2 * HEAD_DEV * LEN
FEW = HEAD_DEV * 8
EARLY = 64
LATE = BLOCK - EARLY
F32 = jnp.float32
BF16 = jnp.bfloat16
FIRST_LIMIT = 56 * 2**20
VMEM_LIMIT = 8 * 2**20
SMEM = pl.BlockSpec(memory_space=pltpu.SMEM)
VMEM = pl.BlockSpec(memory_space=pltpu.VMEM)
ANY = pl.BlockSpec(memory_space=pl.ANY)
HBM = pl.BlockSpec(memory_space=pltpu.HBM)


def estimate(microseconds):
    return pl.CostEstimate(
        flops=0, transcendentals=0, bytes_accessed=int(microseconds * 3.69e6)
    )


def attend_kernel(
    slot_hbm, len_hbm, cache_ref, fresh_hbm, att_ref, kv0, kv1, kv2, kv3,
    slot_scr, len_scr, fresh_scr, held, att_scr, in_sems, sems,
):
    me = lax.axis_index("head")
    row = me // OLD
    lane = me % OLD
    loads = []
    for source, target in (
        (cache_ref.at[0, 0], held.at[0]),
        (fresh_hbm, fresh_scr),
        (slot_hbm, slot_scr),
        (len_hbm, len_scr),
        (cache_ref.at[0, 1], held.at[1]),
    ):
        load = pltpu.make_async_copy(source, target, in_sems.at[len(loads)])
        load.start()
        loads.append(load)
    copies = []

    def pick(kind):
        for offset, kv_ref in ((1, kv1), (2, kv2), (3, kv3), (0, kv0)):
            target = (row + offset) % ROWS
            for i in range(HEAD_DEV):
                slot = slot_scr[(target * OLD + lane) * HEAD_DEV + i]
                at = (kind * HEAD_DEV + i) * LEN
                rows = min(LEN, LATE - at)
                if rows <= 0:
                    continue
                copy = pltpu.make_async_copy(
                    held.at[kind, slot, pl.ds(0, rows)],
                    kv_ref.at[pl.ds(at, rows)],
                    sems.at[len(copies)],
                )
                copy.start()
                copies.append(copy)

    scale = 1.0 / math.sqrt(HEAD_DIM)
    query_rows, old_scores, new_first, new_second = [], [], [], []
    odd = lax.broadcasted_iota(jnp.int32, (8, HEAD_DIM), 0) % 2 == 1
    loads[1].wait()
    fresh = fresh_scr[0].astype(F32)
    for slot in range(SLOTS):
        query = jnp.where(
            odd,
            jnp.broadcast_to(fresh[0, 1, slot : slot + 1], (8, HEAD_DIM)),
            jnp.broadcast_to(fresh[0, 0, slot : slot + 1], (8, HEAD_DIM)),
        )
        query_rows.append(query.astype(BF16))
        new_first.append(jnp.sum(query * fresh[1, 0, slot : slot + 1], axis=-1, keepdims=True))
        new_second.append(jnp.sum(query * fresh[1, 1, slot : slot + 1], axis=-1, keepdims=True))
    loads[0].wait()
    loads[2].wait()
    pick(0)
    for slot in range(SLOTS):
        old_scores.append(
            lax.dot_general(
                query_rows[slot],
                held[0, slot],
                (((1,), (1,)), ((), ())),
                preferred_element_type=F32,
            )
        )
    loads[4].wait()
    pick(1)
    shape = (SLOTS * 8, LEN)
    scores = jnp.concatenate(old_scores, axis=0) * scale
    first = jnp.concatenate(new_first, axis=0) * scale
    second = jnp.concatenate(new_second, axis=0) * scale
    loads[3].wait()
    visible = lax.broadcasted_iota(jnp.int32, shape, 1) < len_scr[row]
    later = lax.broadcasted_iota(jnp.int32, (SLOTS * 8, 1), 0) % 2 == 1
    scores = jnp.where(visible, scores, -1e30)
    second = jnp.where(later, second, -1e30)
    top = jnp.maximum(jnp.max(scores, axis=-1, keepdims=True), jnp.maximum(first, second))
    old_exp = jnp.where(visible, jnp.exp(scores - top), 0.0)
    first_exp = jnp.exp(first - top)
    second_exp = jnp.where(later, jnp.exp(second - top), 0.0)
    total = jnp.sum(old_exp, axis=-1, keepdims=True) + first_exp + second_exp
    old_w = (old_exp / total).astype(BF16)
    first_w = (first_exp / total).astype(BF16).astype(F32)
    second_w = (second_exp / total).astype(BF16).astype(F32)
    mine = lax.broadcasted_iota(jnp.int32, (8, HEAD_DIM), 0) // 2 == row
    for slot in range(SLOTS):
        part = slice(slot * 8, slot * 8 + 8)
        result = jnp.dot(old_w[part], held[1, slot], preferred_element_type=F32)
        result = result + (
            first_w[part] * fresh[2, 0, slot : slot + 1]
            + second_w[part] * fresh[2, 1, slot : slot + 1]
        )
        att_scr[slot] = jnp.where(mine, result, 0.0)
    for target in range(ROWS):
        pair = [
            att_scr[slot_scr[(target * OLD + lane) * HEAD_DEV + i]] for i in range(HEAD_DEV)
        ]
        att_ref[LINE_RANK[target], :FEW] = jnp.concatenate(pair, axis=0).astype(BF16)
        slot = slot_scr[(target * OLD + lane) * HEAD_DEV + HEAD_DEV - 1]
        att_ref[LINE_RANK[target], FEW:] = held[1, slot, LEN - EARLY :]
    for copy in copies:
        copy.wait()


def attend_and_pick(slot_map, lengths, cache, fresh):
    return pl.pallas_call(
        attend_kernel,
        out_shape=(
            jax.ShapeDtypeStruct((ROWS, FEW + EARLY, HEAD_DIM), BF16),
            *[jax.ShapeDtypeStruct((LATE, HEAD_DIM), BF16)] * ROWS,
        ),
        in_specs=[ANY] * 4,
        out_specs=(VMEM, *[ANY] * ROWS),
        scratch_shapes=[
            pltpu.SMEM(slot_map.shape, jnp.int32),
            pltpu.SMEM(lengths.shape, jnp.int32),
            pltpu.VMEM(fresh.shape, BF16),
            pltpu.VMEM((2, SLOTS, LEN, HEAD_DIM), BF16),
            pltpu.VMEM((SLOTS, 8, HEAD_DIM), F32),
            pltpu.SemaphoreType.DMA((5,)),
            pltpu.SemaphoreType.DMA((ROWS * HEAD_DEV * 2,)),
        ],
        cost_estimate=estimate(3.5),
        compiler_params=pltpu.CompilerParams(vmem_limit_bytes=FIRST_LIMIT),
        name="attend_and_pick",
    )(slot_map, lengths, cache, fresh)


def touch_kernel(weight_ref, out_ref):
    out_ref[...] = jnp.zeros_like(out_ref)


def touch(out_weight):
    return pl.pallas_call(
        touch_kernel,
        out_shape=jax.ShapeDtypeStruct((16, 128), BF16),
        in_specs=[ANY],
        out_specs=VMEM,
        cost_estimate=estimate(0.2),
        compiler_params=pltpu.CompilerParams(vmem_limit_bytes=VMEM_LIMIT),
        name="touch",
    )(out_weight)


def project_kernel(att_ref, weight_ref, *refs):
    out_ref = refs[-1]
    total = att_ref[0, :FEW].astype(F32)
    for row in range(1, ROWS):
        total = total + att_ref[row, :FEW].astype(F32)
    features = jnp.concatenate([total[:8], total[8:]], axis=1).astype(BF16)
    for chip in range(CHIPS):
        part = jnp.dot(
            features,
            weight_ref[:, chip * CHUNK : (chip + 1) * CHUNK],
            preferred_element_type=F32,
        )
        out_ref[SUM_RANK[chip]] = part.astype(BF16)


def project(attended, out_weight, *arrived):
    return pl.pallas_call(
        project_kernel,
        out_shape=jax.ShapeDtypeStruct((CHIPS, 8, CHUNK), BF16),
        in_specs=[VMEM, VMEM] + [ANY] * len(arrived),
        out_specs=VMEM,
        cost_estimate=estimate(0.6),
        compiler_params=pltpu.CompilerParams(vmem_limit_bytes=VMEM_LIMIT),
        name="project",
    )(attended, out_weight, *arrived)


def widen_kernel(residual_ref, out_ref):
    core = lax.axis_index("head") % CORES
    own = jnp.concatenate([residual_ref[row].astype(F32) for row in range(ROWS)], axis=0)
    none = jnp.zeros_like(own)
    out_ref[...] = jnp.concatenate(
        [jnp.where(core == 0, own, none), jnp.where(core == 1, own, none)], axis=1
    )


def widen(residual):
    return pl.pallas_call(
        widen_kernel,
        out_shape=jax.ShapeDtypeStruct((8, CHUNK), F32),
        in_specs=[VMEM],
        out_specs=VMEM,
        cost_estimate=estimate(0.7),
        compiler_params=pltpu.CompilerParams(vmem_limit_bytes=VMEM_LIMIT),
        name="widen",
    )(residual)


def add_kernel(parts_ref, residual_ref, out_ref):
    total = parts_ref[0].astype(F32)
    for chip in range(1, CHIPS):
        total = total + parts_ref[chip].astype(F32)
    out_ref[...] = total + residual_ref[...]


def add_residual(parts, residual):
    return pl.pallas_call(
        add_kernel,
        out_shape=jax.ShapeDtypeStruct((8, CHUNK), F32),
        in_specs=[VMEM, VMEM],
        out_specs=VMEM,
        cost_estimate=estimate(0.2),
        compiler_params=pltpu.CompilerParams(vmem_limit_bytes=VMEM_LIMIT),
        name="add_residual",
    )(parts, residual)


def hidden_kernel(sums_ref, spread_ref):
    hidden = (sums_ref[0] + sums_ref[1]).astype(BF16)
    for chip in range(CHIPS):
        spread_ref[chip] = hidden


def round_hidden(sums):
    return pl.pallas_call(
        hidden_kernel,
        out_shape=jax.ShapeDtypeStruct((CHIPS, 8, CHUNK), BF16),
        in_specs=[VMEM],
        out_specs=VMEM,
        cost_estimate=estimate(0.2),
        compiler_params=pltpu.CompilerParams(vmem_limit_bytes=VMEM_LIMIT),
        name="round_hidden",
    )(sums)


def place(offsets, refs, cache_ref, sems):
    row = lax.axis_index("head") // OLD
    copies = []
    for offset, ref in zip(offsets, refs):
        source = (row + ROWS - offset) % ROWS
        for part in (pl.ds(0, BLOCK // 2), pl.ds(BLOCK // 2, LATE - BLOCK // 2)):
            copy = pltpu.make_async_copy(
                ref.at[part], cache_ref.at[0, source, part], sems.at[len(copies)]
            )
            copy.start()
            copies.append(copy)
    return copies


def norm_kernel(offsets, blocks_ref, gain_ref, bias_ref, early_ref, *refs):
    *kv_refs, out_ref, hidden_ref, cache_ref, sems = refs
    copies = place(offsets, kv_refs, cache_ref, sems)
    for row in range(ROWS):
        copy = pltpu.make_async_copy(
            early_ref.at[LINE_RANK[row], pl.ds(FEW, EARLY)],
            cache_ref.at[0, row, pl.ds(LATE, EARLY)],
            sems.at[len(copies)],
        )
        copy.start()
        copies.append(copy)
    me = lax.axis_index("head")
    chip = me // CORES
    own = jnp.zeros((8, CHUNK), F32)
    for one in range(CHIPS):
        own = jnp.where(chip == one, blocks_ref[ROW_RANK[one]].astype(F32), own)
    own = jnp.where(me % CORES == 0, own[:, :SHARE], own[:, SHARE:]).astype(BF16)
    for step in range(ROWS):
        hidden_ref[step] = own[2 * step : 2 * step + 2]
    total = blocks_ref[0].astype(F32)
    for chip in range(1, CHIPS):
        total = total + blocks_ref[chip].astype(F32)
    mean = jnp.sum(total, axis=-1, keepdims=True) / OUT
    spread = jnp.zeros((8, CHUNK), F32)
    for chip in range(CHIPS):
        spread = spread + (blocks_ref[chip].astype(F32) - mean) ** 2
    var = jnp.sum(spread, axis=-1, keepdims=True) / OUT
    scale = 1.0 / jnp.sqrt(var + 1e-05)
    tiles = CHUNK // 128
    for chip in range(CHIPS):
        values = (blocks_ref[ROW_RANK[chip]].astype(F32) - mean) * scale
        for tile in range(tiles):
            at = chip * tiles + tile
            part = values[:, tile * 128 : (tile + 1) * 128]
            part = (part * gain_ref[at : at + 1] + bias_ref[at : at + 1]).astype(BF16)
            for step in range(ROWS):
                out_ref[step, :, at * 128 : (at + 1) * 128] = part[2 * step : 2 * step + 2]
    for copy in copies:
        copy.wait()


def normalize(blocks, gain, bias, early, offsets, kv):
    return pl.pallas_call(
        functools.partial(norm_kernel, offsets),
        out_shape=(
            jax.ShapeDtypeStruct((ROWS, 2, OUT), BF16),
            jax.ShapeDtypeStruct((ROWS, 2, SHARE), BF16),
            jax.ShapeDtypeStruct((1, ROWS, BLOCK, HEAD_DIM), BF16),
        ),
        in_specs=[VMEM] * (4 + len(kv)),
        out_specs=(VMEM, VMEM, HBM),
        scratch_shapes=[pltpu.SemaphoreType.DMA((2 * len(kv) + ROWS,))],
        cost_estimate=estimate(1.4),
        compiler_params=pltpu.CompilerParams(vmem_limit_bytes=VMEM_LIMIT),
        name="normalize",
    )(
        blocks,
        gain.reshape(OUT // 128, 128),
        bias.reshape(OUT // 128, 128),
        early,
        *kv,
    )


def last_kernel(offset, block_ref, _, cache_ref, sems):
    for copy in place((offset,), (block_ref,), cache_ref, sems):
        copy.wait()


def place_last(offset, block, cache_new):
    return pl.pallas_call(
        functools.partial(last_kernel, offset),
        out_shape=jax.ShapeDtypeStruct(cache_new.shape, BF16),
        in_specs=[VMEM, HBM],
        out_specs=HBM,
        scratch_shapes=[pltpu.SemaphoreType.DMA((2,))],
        input_output_aliases={1: 0},
        cost_estimate=estimate(0.6),
        compiler_params=pltpu.CompilerParams(vmem_limit_bytes=VMEM_LIMIT),
        name="place_last",
    )(block, cache_new)


def exchange(blocks, groups):
    return lax.all_to_all(blocks, "head", 0, 0, axis_index_groups=groups, tiled=True)


def body(cache, fresh, slot_map, lengths, out_weight, residual, norm_gain, norm_bias):
    columns = [[row * OLD + lane for row in LINE_ORDER] for lane in range(OLD)]
    sum_sides = [[chip * CORES + core for chip in SUM_ORDER] for core in range(CORES)]
    row_sides = [[chip * CORES + core for chip in ROW_ORDER] for core in range(CORES)]
    pairs = [[chip * CORES + core for core in range(CORES)] for chip in range(CHIPS)]
    picked, *kv = attend_and_pick(slot_map, lengths, cache, fresh)
    first, inner = 1, (2, 3)

    def shifted(offset):
        pairs = [(i, (i + offset * OLD) % MEMBERS) for i in range(MEMBERS)]
        return lax.ppermute(kv[offset], "head", pairs)

    def region(run, *operands):
        def none(*operands):
            return jax.tree.map(lambda t: jnp.zeros(t.shape, t.dtype), jax.eval_shape(run, *operands))

        return lax.cond(lax.axis_index("head") < MEMBERS, run, none, *operands)

    def finish(total):
        sums = lax.all_gather(total, "head", axis_index_groups=pairs)
        return exchange(round_hidden(sums), row_sides)

    def middle(attended, weight, residual, gain, bias, *seen):
        parts = exchange(project(attended, weight, *seen), sum_sides)
        moved = [shifted(offset) for offset in inner]
        blocks = region(finish, add_residual(parts, widen(residual)))
        return normalize(blocks, gain, bias, attended, (0,) + inner, (kv[0], *moved))

    moved = shifted(first)
    attended = exchange(picked, columns)
    normed, hidden, cache_new = region(
        middle, attended, out_weight, residual, norm_gain, norm_bias, touch(out_weight)
    )
    cache_new = place_last(first, moved, cache_new)
    return (cache_new.reshape(1, ROWS, 2, HEAD_DEV, LEN, HEAD_DIM), hidden, normed)


def solution(mesh):
    in_specs = (
        P(("grp", "head"), None, None, None, None),
        P(("grp", "head"), None, None, None, None),
        P("grp"),
        P("grp"),
        P("head", None),
        P("grp", None, "head"),
        P(),
        P(),
    )
    out_specs = (
        P(("grp", "head"), None, None, None, None, None),
        P("grp", None, "head"),
        P("grp", None, None),
    )
    return jax.shard_map(body, mesh=mesh, in_specs=in_specs, out_specs=out_specs, check_vma=False)
```
